128 devices in a mesh: dp: 16 (over y_lo, z, core), tensor: 8 (over x, y_hi).
Axes of the slice: x: 4, y: 4 (y_hi: 2, y_lo: 2; y = y_hi * 2 + y_lo), z: 4, core: 2. Of those that a mesh axis runs over, the one named last changes fastest.
Arguments:
- tokens: bfloat16 [16384, 1024], P(('dp', 'tensor')), may hold values from -6 to 6
- cotangent: bfloat16 [16384, 1024], P(('dp', 'tensor')), may hold values from -6 to 6
- w_query: bfloat16 [1024, 2048], P('dp', 'tensor'), may hold values from -0.1875 to 0.1875
- w_key: bfloat16 [1024, 1024], P('dp', 'tensor'), may hold values from -0.1875 to 0.1875
- w_value: bfloat16 [1024, 1024], P('dp', 'tensor'), may hold values from -0.1875 to 0.1875
- w_output: bfloat16 [1024, 2048], P('dp', 'tensor'), may hold values from -1.5 to 1.5
- w_gate: bfloat16 [1024, 3072], P('dp', 'tensor'), may hold values from -0.1875 to 0.1875
- w_up: bfloat16 [1024, 3072], P('dp', 'tensor'), may hold values from -0.1875 to 0.1875
- w_down: bfloat16 [1024, 3072], P('dp', 'tensor'), may hold values from -0.109375 to 0.109375
- norm_attn: float32 [1024], replicated, may hold values from 0.25 to 1.75
- norm_mlp: float32 [1024], replicated, may hold values from 0.25 to 1.75
- query_norm: float32 [128], replicated, may hold values from 0.25 to 1.75
- key_norm: float32 [128], replicated, may hold values from 0.25 to 1.75
- segment: int32 [16384], P(('dp', 'tensor')), may hold values from 0 to 3, as said below
- position: int32 [16384], P(('dp', 'tensor')), may hold values from 0 to 799, as said below
Outputs:
- mixed: bfloat16 [16384, 1024], P(('dp', 'tensor'))
- grad_tokens: bfloat16 [16384, 1024], P(('dp', 'tensor'))
- grad_query: float32 [1024, 2048], P('dp', 'tensor')
- grad_key: float32 [1024, 1024], P('dp', 'tensor')
- grad_value: float32 [1024, 1024], P('dp', 'tensor')
- grad_output: float32 [1024, 2048], P('dp', 'tensor')
- grad_gate: float32 [1024, 3072], P('dp', 'tensor')
- grad_up: float32 [1024, 3072], P('dp', 'tensor')
- grad_down: float32 [1024, 3072], P('dp', 'tensor')
- grad_norm_attn: float32 [1024], replicated
- grad_norm_mlp: float32 [1024], replicated
- grad_query_norm: float32 [128], replicated
- grad_key_norm: float32 [128], replicated
The draws below stay inside these ranges and needn't reach their ends.
Inputs may be any that keep to these rules, and one draw needn't show every extreme that they name: Within each sequence (tokens s * 1024 to s * 1024 + 1023) segment numbers start at 0, never fall and rise by one at each new document; a sequence holds three or four documents of 60 to 800 tokens; tokens of different sequences never attend to one another. A token's position is its offset from the first token of its document, the run of equal segment numbers that holds it.
All inputs are finite; a program needn't handle non-finite values.
Results may differ from the reference program's by a relative error of at most 0.022.
Values may be sent and summed in bfloat16 or wider, within the bound.
No kernel may reach another device: no remote copies, remote signals or barrier semaphores. Data moves between devices by JAX's collectives and lax.ppermute only.
A program may use at most 128 MiB of HBM per device.

```python
import math
import jax
import jax.numpy as jnp
from jax import lax

D = 1024
HQ = 16
HK = 8
HD = 128
FF = 3072
LEN = 1024
TOKENS = 16384


def document_layout(key):
    seq_count = TOKENS // LEN
    min_doc = LEN * 15 // 256
    max_doc = LEN * 25 // 32
    rest_rows = LEN - max_doc
    lowest = LEN // 8 - LEN // 32 + 1
    highest = rest_rows - min_doc
    first_lowest = max(lowest, 2 * min_doc)
    start_key = jax.random.fold_in(key, 11)
    first_key = jax.random.fold_in(key, 13)
    cut_key = jax.random.fold_in(key, 17)
    starts = jax.random.randint(start_key, (seq_count,), lowest, highest + 1).astype(jnp.int32)
    first_start = jax.random.randint(first_key, (seq_count,), first_lowest, highest + 1).astype(jnp.int32)
    seq_index = jnp.arange(seq_count, dtype=jnp.int32)
    starts = jnp.where(seq_index == 0, first_start, starts)
    splits = starts >= 2 * min_doc
    spans = jnp.maximum(starts - 2 * min_doc + 1, 1)
    cuts = min_doc + jax.random.randint(cut_key, (seq_count,), 0, 1 << 20).astype(jnp.int32) % spans
    cuts = jnp.where(splits, cuts, starts)
    row_index = jnp.arange(LEN, dtype=jnp.int32)[None, :]
    split_cut = cuts[:, None]
    long_start = starts[:, None]
    long_end = long_start + max_doc
    split_flag = splits[:, None].astype(jnp.int32)
    seg_ids = (row_index >= split_cut).astype(jnp.int32) * split_flag + (row_index >= long_start).astype(jnp.int32) + (row_index >= long_end).astype(jnp.int32)
    doc_start = jnp.zeros((seq_count, LEN), jnp.int32)
    doc_start = jnp.where((row_index >= split_cut) & (split_flag == 1), split_cut, doc_start)
    doc_start = jnp.where(row_index >= long_start, long_start, doc_start)
    doc_start = jnp.where(row_index >= long_end, long_end, doc_start)
    return (seg_ids.reshape(-1).astype(jnp.int32), (row_index - doc_start).reshape(-1).astype(jnp.int32))


def draw_segment(key, part):
    seg_ids, offsets = document_layout(key)
    return seg_ids


def draw_position(key, part):
    seg_ids, offsets = document_layout(key)
    return offsets


def block_levels(key, extent, cuts, least, top_value):
    def one(dim, shards_of):
        heights = jax.random.uniform(jax.random.fold_in(jax.random.fold_in(key, 6), dim), (shards_of,), jnp.float32, least / len(cuts), top_value / len(cuts))
        return jnp.repeat(jnp.exp(heights), extent[dim] // shards_of).reshape((-1,) + (1,) * (len(extent) - dim - 1))

    loudness = one(*cuts[0])
    for cut in cuts[1:]:
        loudness = loudness * one(*cut)
    return loudness


def noise(own_key, dims, scale, limit, pieces=(), held_as=jnp.bfloat16):
    gain = block_levels(own_key, dims, pieces, -0.22, 0.18) if pieces else 1.0
    result = jax.random.normal(own_key, dims, jnp.float32) * scale * gain
    return jnp.minimum(jnp.maximum(result, -limit), limit).astype(held_as)


def setup_inputs(seed: int = 0) -> dict:
    arg_keys = jax.random.split(jax.random.key(seed), 16)
    return {
        "tokens": noise(arg_keys[0], (TOKENS, D), 1.0, 6.0, ((0, 128),)),
        "cotangent": noise(arg_keys[1], (TOKENS, D), 1.0, 6.0, ((0, 128),)),
        "w_query": noise(arg_keys[2], (D, HQ * HD), D ** -0.5, 0.1875, ((0, 16), (1, 8))),
        "w_key": noise(arg_keys[3], (D, HK * HD), D ** -0.5, 0.1875, ((0, 16), (1, 8))),
        "w_value": noise(arg_keys[4], (D, HK * HD), D ** -0.5, 0.1875, ((0, 16), (1, 8))),
        "w_output": noise(arg_keys[5], (D, HQ * HD), (HQ * HD // 128) ** -0.5, 1.5, ((0, 16), (1, 8))),
        "w_gate": noise(arg_keys[6], (D, FF), D ** -0.5, 0.1875, ((0, 16), (1, 8))),
        "w_up": noise(arg_keys[7], (D, FF), D ** -0.5, 0.1875, ((0, 16), (1, 8))),
        "w_down": noise(arg_keys[8], (D, FF), FF ** -0.5, 0.109375, ((0, 16), (1, 8))),
        "norm_attn": jnp.clip(1.0 + 0.15 * jax.random.normal(arg_keys[9], (D,), jnp.float32), 0.25, 1.75),
        "norm_mlp": jnp.clip(1.0 + 0.15 * jax.random.normal(arg_keys[10], (D,), jnp.float32), 0.25, 1.75),
        "query_norm": jnp.clip(1.0 + 0.15 * jax.random.normal(arg_keys[11], (HD,), jnp.float32), 0.25, 1.75),
        "key_norm": jnp.clip(1.0 + 0.15 * jax.random.normal(arg_keys[12], (HD,), jnp.float32), 0.25, 1.75),
        "segment": draw_segment(jax.random.fold_in(arg_keys[15], 71), 0),
        "position": draw_position(jax.random.fold_in(arg_keys[15], 71), 0),
    }


eps_norm = 1e-06
rope_base = 1000000.0
masked_score = -1e+30

@jax.custom_vjp
def low(v):
    return lax.optimization_barrier(v.astype(jnp.bfloat16)).astype(jnp.float32)

@jax.custom_vjp
def low_back(v):
    return v

def low_keep(v):
    return (low(v), None)

def low_pass(kept, grad):
    return (grad,)

def back_keep(v):
    return (v, None)

def back_low(kept, grad):
    return (low(grad),)
low.defvjp(low_keep, low_pass)
low_back.defvjp(back_keep, back_low)

def product(left_side, right_side):
    return jnp.dot(left_side, right_side, precision=lax.Precision.HIGHEST, preferred_element_type=jnp.float32)

def rms_scale(values, gain_vector):
    return values * lax.rsqrt(lax.optimization_barrier(jnp.mean(values * values, axis=-1, keepdims=True)) + eps_norm) * gain_vector

def rotary_tables(positions):
    half_size = HD // 2
    frequency = jnp.power(rope_base, -2.0 * jnp.arange(half_size, dtype=jnp.float32) / HD)
    angles = positions.astype(jnp.float32)[:, None, None] * frequency
    return (jnp.cos(angles), jnp.sin(angles))

def rotate_pairs(values, cosine, sine_table):
    half_size = values.shape[-1] // 2
    former = values[..., :half_size]
    latter = values[..., half_size:]
    return jnp.concatenate([former * cosine - latter * sine_table, latter * cosine + former * sine_table], axis=-1)

def attend_sequence(sequence_items):
    queries, key_rows, values, segments, positions = sequence_items
    grouped = queries.reshape(LEN, HK, HQ // HK, HD)
    raw_scores = jnp.einsum('qhgd,khd->hgqk', grouped, key_rows, precision=lax.Precision.HIGHEST)
    scores = low_back(raw_scores) * (1.0 / math.sqrt(HD))
    allowed = (segments[:, None] == segments[None, :]) & (positions[None, :] <= positions[:, None])
    scores = jnp.where(allowed, scores, masked_score)
    expo_scores = jnp.exp(scores - lax.optimization_barrier(jnp.max(scores, axis=-1, keepdims=True)))
    weights = low(expo_scores / lax.optimization_barrier(jnp.sum(expo_scores, axis=-1, keepdims=True)))
    mixed_rows = jnp.einsum('hgqk,khd->qhgd', weights, values, precision=lax.Precision.HIGHEST)
    return low(low_back(mixed_rows)).reshape(LEN, HQ * HD)

def layer(tokens, w_query, w_key, w_value, w_output, w_gate, w_up, w_down, norm_attn, norm_mlp, query_norm, key_norm, segment, position):
    normed = low(rms_scale(tokens, norm_attn))
    query_raw = low_back(product(normed, w_query))
    key_raw = low_back(product(normed, w_key))
    value_rows = low(low_back(product(normed, w_value)))
    cosine, sine_table = rotary_tables(position)
    queries = low(rotate_pairs(rms_scale(query_raw.reshape(-1, HQ, HD), query_norm), cosine, sine_table))
    key_rows = low(rotate_pairs(rms_scale(key_raw.reshape(-1, HK, HD), key_norm), cosine, sine_table))
    seq_count = TOKENS // LEN
    attended = lax.map(jax.checkpoint(attend_sequence), (queries.reshape(seq_count, LEN, HQ * HD), key_rows.reshape(seq_count, LEN, HK, HD), value_rows.reshape(seq_count, LEN, HK, HD), segment.reshape(seq_count, LEN), position.reshape(seq_count, LEN)))
    attn_out = low_back(product(attended.reshape(-1, HQ * HD), w_output.T))
    middle = tokens + attn_out
    normed_mlp = low(rms_scale(middle, norm_mlp))
    gate_rows = low_back(product(normed_mlp, w_gate))
    upward = low_back(product(normed_mlp, w_up))
    active = low(gate_rows / (1.0 + jnp.exp(-gate_rows)) * upward)
    return middle + low_back(product(active, w_down.T))

def reference(tokens, cotangent, w_query, w_key, w_value, w_output, w_gate, w_up, w_down, norm_attn, norm_mlp, query_norm, key_norm, segment, position):
    floats = tuple((operand.astype(jnp.float32) for operand in (tokens, w_query, w_key, w_value, w_output, w_gate, w_up, w_down, norm_attn, norm_mlp, query_norm, key_norm)))

    def forward(*arrays):
        return layer(*arrays, segment, position)
    output, pullback = jax.vjp(forward, *floats)
    gradients = pullback(cotangent.astype(jnp.float32))
    return (output.astype(jnp.bfloat16), gradients[0].astype(jnp.bfloat16), gradients[1], gradients[2], gradients[3], gradients[4], gradients[5], gradients[6], gradients[7], gradients[8], gradients[9], gradients[10], gradients[11])
```

```python
import itertools
import math

import jax
import jax.numpy as jnp
from jax import lax
from jax.experimental import pallas as pl
from jax.experimental.pallas import tpu as pltpu
from jax.sharding import Mesh
from jax.sharding import PartitionSpec as P

HD = 128
LEN = 1024
BLK = 128

eps_norm = 1e-06
rope_base = 1000000.0
masked_score = -1e30
scale = 1.0 / math.sqrt(HD)

BF = jnp.bfloat16
F32 = jnp.float32

AXES = ("yl", "z", "c", "x", "yh")
SIZES = {"yl": 2, "z": 4, "c": 2, "x": 4, "yh": 2}


def pairs(axes, move):
    sizes = [SIZES[a] for a in axes]
    out = []
    for place in itertools.product(*[range(s) for s in sizes]):
        target = move(dict(zip(axes, place)))
        source = goal = 0
        for a, s, v in zip(axes, sizes, place):
            source = source * s + v
            goal = goal * s + target[a]
        out.append((source, goal))
    return out


def send(value, **flips):
    axes = tuple(a for a in AXES if a in flips)
    table = pairs(axes, lambda p: {a: p[a] ^ flips[a] for a in axes})
    return lax.ppermute(value, axes if len(axes) > 1 else axes[0], table)


def matmul(left, right):
    return jnp.dot(left, right, preferred_element_type=F32)


def times_transposed(left, right):
    return lax.dot_general(left, right, (((1,), (1,)), ((), ())), preferred_element_type=F32)


def transposed_times(left, right):
    return lax.dot_general(left, right, (((0,), (0,)), ((), ())), preferred_element_type=F32)


def gather_tokens(rows):
    own = jnp.concatenate([rows] + [send(rows, x=k) for k in (1, 3, 2)])
    return own, send(own, c=1)


def scatter_tokens(own, other):
    count = own.shape[0] // 4
    total = own + send(other.astype(BF), c=1).astype(F32)
    low = total.astype(BF)
    out = total[:count]
    for i, k in enumerate((1, 3, 2)):
        out = out + send(low[(i + 1) * count : (i + 2) * count], x=k).astype(F32)
    return out


def swap_shards(value):
    axes = ("c", "yh")
    return lax.ppermute(value, axes, pairs(axes, lambda p: {"c": p["yh"], "yh": p["c"]}))


def reorder(blocks, order):
    count, rows, columns = blocks.shape

    def body(order_ref, in_ref, out_ref):
        out_ref[...] = in_ref[...]

    return pl.pallas_call(
        body,
        grid_spec=pltpu.PrefetchScalarGridSpec(
            num_scalar_prefetch=1,
            grid=(count,),
            in_specs=[pl.BlockSpec((1, rows, columns), lambda i, order_ref: (order_ref[i], 0, 0))],
            out_specs=pl.BlockSpec((1, rows, columns), lambda i, order_ref: (i, 0, 0)),
        ),
        out_shape=jax.ShapeDtypeStruct(blocks.shape, blocks.dtype),
        cost_estimate=pl.CostEstimate(flops=0, bytes_accessed=4 * blocks.size, transcendentals=0),
    )(order, blocks)


def gather_weights(shard):
    axes = ("yl", "c", "yh")
    got = []
    for k1 in range(2):
        for k2 in range(2):
            table = pairs(
                axes, lambda p: {"c": p["yh"], "yl": p["yl"] ^ k2, "yh": p["c"] ^ k1}
            )
            got.append(lax.ppermute(shard, axes, table))
    plane = jnp.stack(got)
    whole = jnp.concatenate([plane] + [send(plane, z=k) for k in (1, 3, 2)])
    yl, z, yh = (lax.axis_index(a) for a in ("yl", "z", "yh"))
    slot_of = jnp.array([0, 1, 3, 2], jnp.int32)
    place = jnp.arange(16, dtype=jnp.int32)
    from_yl, from_z, from_c = place // 8, (place // 2) % 4, place % 2
    order = slot_of[from_z ^ z] * 4 + (from_c ^ yh) * 2 + (from_yl ^ yl)
    return reorder(whole, order).reshape(-1, shard.shape[1])


def rms_inverse(values):
    return lax.rsqrt(jnp.mean(values * values, axis=-1, keepdims=True) + eps_norm)


def rms_backward(grad_rows, values, inverse, gain):
    scaled = grad_rows * gain
    return inverse * (
        scaled - values * inverse * inverse * jnp.mean(scaled * values, axis=-1, keepdims=True)
    )


def swapped_halves(values):
    return jnp.concatenate([values[:, HD // 2 :], values[:, : HD // 2]], axis=1)


def head_forward(raw, gain, cosine, sine):
    unit = raw * rms_inverse(raw) * gain
    return (unit * cosine + swapped_halves(unit) * sine).astype(BF)


def head_backward(grad, raw, gain, cosine, sine):
    inverse = rms_inverse(raw)
    back = grad * cosine - swapped_halves(grad) * sine
    gain_part = jnp.sum(back * raw * inverse, axis=0)
    return rms_backward(back, raw, inverse, gain).astype(BF), gain_part


def allowed_keys(index_rows, position_rows, key_index):
    first = index_rows - position_rows
    return (key_index[None, :] <= index_rows[:, None]) & (key_index[None, :] >= first[:, None])


def attend(queries, keys, values, allowed):
    scores = jnp.where(allowed, times_transposed(queries, keys) * scale, masked_score)
    top = jnp.max(scores, axis=-1, keepdims=True)
    expo = jnp.exp(scores - top)
    total = jnp.sum(expo, axis=-1, keepdims=True)
    weights = (expo / total).astype(BF)
    return matmul(weights, values).astype(BF), top, total


def attend_backward(queries, keys, values, allowed, top, total, grad):
    scores = jnp.where(allowed, times_transposed(queries, keys) * scale, masked_score)
    weights = jnp.exp(scores - top) / total
    grad_values = transposed_times(weights.astype(BF), grad)
    grad_weights = times_transposed(grad, values)
    grad_scores = weights * (
        grad_weights - jnp.sum(weights * grad_weights, axis=-1, keepdims=True)
    )
    low = (grad_scores * scale).astype(BF)
    return matmul(low, keys), transposed_times(low, queries), grad_values


def shards(
    tokens,
    cotangent,
    w_query,
    w_key,
    w_value,
    w_output,
    w_gate,
    w_up,
    w_down,
    norm_attn,
    norm_mlp,
    query_norm,
    key_norm,
    segment,
    position,
):
    x, yh = lax.axis_index("x"), lax.axis_index("yh")

    w_qkv = gather_weights(jnp.concatenate([w_query, w_key, w_value], axis=1))
    rest = swap_shards(jnp.concatenate([w_output, w_gate, w_up, w_down], axis=1))
    rest = lax.all_gather(rest, ("yh", "yl", "z"), axis=0)
    rest = rest.reshape(2, 8, 64, -1).transpose(1, 0, 2, 3).reshape(1024, -1)
    w_out, w_gu, w_dn = rest[:, :256], rest[:, 256:1024], rest[:, 1024:]

    local_rows = tokens.astype(F32)
    inverse_one = rms_inverse(local_rows)
    normed = (local_rows * inverse_one * norm_attn).astype(BF)
    high = position // 32
    extra = jnp.stack([high, position - 32 * high]).astype(BF)
    extra = jnp.pad(extra, ((0, 6), (0, 1024 - BLK)))
    gathered = gather_tokens(jnp.concatenate([normed, extra]))
    normed_rows, positions = [], []
    for part in gathered:
        part = part.reshape(4, BLK + 8, 1024)
        normed_rows.append(part[:, :BLK].reshape(4 * BLK, 1024))
        marks = part[:, BLK : BLK + 2, :BLK].astype(jnp.int32)
        positions.append((marks[:, 0] * 32 + marks[:, 1]).reshape(-1))
    cot_rows = gather_tokens(cotangent)

    frequency = jnp.power(rope_base, -2.0 * jnp.arange(HD // 2, dtype=F32) / HD)
    rope = []
    for position_rows in positions:
        angles = position_rows.astype(F32)[:, None] * frequency
        cosine, sine = jnp.cos(angles), jnp.sin(angles)
        rope.append(
            (jnp.concatenate([cosine, cosine], 1), jnp.concatenate([-sine, sine], 1))
        )
    raw = [matmul(rows, w_qkv) for rows in normed_rows]
    query_raw = [[r[:, :HD], r[:, HD : 2 * HD]] for r in raw]
    key_raw = [r[:, 2 * HD : 3 * HD] for r in raw]
    value_own = [r[:, 3 * HD :].astype(BF) for r in raw]
    key_own = [head_forward(k, key_norm, *t) for k, t in zip(key_raw, rope)]
    queries = [[head_forward(q, query_norm, *t) for q in qs] for qs, t in zip(query_raw, rope)]
    key_value = jnp.concatenate([jnp.concatenate([k, v], 1) for k, v in zip(key_own, value_own)])
    far = send(key_value, yh=1).reshape(2, 4 * BLK, 2 * HD)
    keys = [jnp.concatenate([k, far[i, :, :HD]]) for i, k in enumerate(key_own)]
    values = [jnp.concatenate([v, far[i, :, HD:]]) for i, v in enumerate(value_own)]

    inside = jnp.arange(BLK, dtype=jnp.int32)
    block_x = x ^ jnp.array([0, 1, 3, 2], jnp.int32)
    index_rows = ((2 * block_x + yh)[:, None] * BLK + inside).reshape(-1)
    index_far = ((2 * block_x + 1 - yh)[:, None] * BLK + inside).reshape(-1)
    key_index = jnp.concatenate([index_rows, index_far])
    allowed = [allowed_keys(index_rows, p, key_index) for p in positions]
    attended, stats = [], []
    for i in range(2):
        heads = [attend(q, keys[i], values[i], allowed[i]) for q in queries[i]]
        attended.append(jnp.concatenate([h[0] for h in heads], 1))
        stats.append([h[1:] for h in heads])
    attn_part = [times_transposed(a, w_out) for a in attended]
    middle = local_rows + scatter_tokens(*attn_part)

    inverse_two = rms_inverse(middle)
    normed_two = (middle * inverse_two * norm_mlp).astype(BF)
    mlp_rows = gather_tokens(normed_two)
    grad_active = [matmul(c, w_dn) for c in cot_rows]
    active, grad_gu = [], []
    for rows, grad in zip(mlp_rows, grad_active):
        gate_up = matmul(rows, w_gu)
        gate, up = gate_up[:, :384], gate_up[:, 384:]
        sigmoid = 1.0 / (1.0 + jnp.exp(-gate))
        silu = gate * sigmoid
        active.append((silu * up).astype(BF))
        grad_gu.append(
            jnp.concatenate(
                [
                    (grad * up * sigmoid * (1.0 + gate * (1.0 - sigmoid))).astype(BF),
                    (grad * silu).astype(BF),
                ],
                axis=1,
            )
        )
    grad_normed_two = scatter_tokens(*[times_transposed(g, w_gu) for g in grad_gu])
    mlp_out = scatter_tokens(*[times_transposed(a, w_dn) for a in active])
    result = (middle + mlp_out).astype(BF)
    grad_wgu = transposed_times(jnp.concatenate(mlp_rows), jnp.concatenate(grad_gu))
    grad_wdn = transposed_times(jnp.concatenate(cot_rows), jnp.concatenate(active))
    gain_two = jnp.sum(grad_wgu * w_gu.astype(F32), axis=1) / norm_mlp
    mlp_grads = jnp.concatenate([grad_wgu, grad_wdn], 1).astype(BF)
    mlp_grads = mlp_grads.reshape(8, 2, 64, -1).transpose(1, 0, 2, 3).reshape(1024, -1)
    mlp_grads = lax.psum_scatter(mlp_grads, ("yh", "yl", "z"), scatter_dimension=0, tiled=True)
    mlp_grads = swap_shards(mlp_grads).astype(F32)

    grad_middle = cotangent.astype(F32) + rms_backward(
        grad_normed_two, middle, inverse_two, norm_mlp
    )
    grad_attn = gather_tokens(grad_middle.astype(BF))
    grad_attended = [matmul(g, w_out).astype(BF) for g in grad_attn]
    query_grads, query_gain, own_grads, far_grads = [], 0.0, [], []
    for i in range(2):
        low_grads, key_sum, value_sum = [], 0.0, 0.0
        for h in range(2):
            grad_query, grad_key, grad_value = attend_backward(
                queries[i][h],
                keys[i],
                values[i],
                allowed[i],
                *stats[i][h],
                grad_attended[i][:, h * HD : (h + 1) * HD],
            )
            low, gain_part = head_backward(grad_query, query_raw[i][h], query_norm, *rope[i])
            low_grads.append(low)
            query_gain = query_gain + gain_part
            key_sum, value_sum = key_sum + grad_key, value_sum + grad_value
        query_grads.append(low_grads)
        both = jnp.concatenate([key_sum, value_sum], 1)
        own_grads.append(both[: 4 * BLK])
        far_grads.append(both[4 * BLK :])
    got = send(jnp.concatenate(far_grads).astype(BF), yh=1).astype(F32)
    grad_qkv, key_gain = [], 0.0
    for i in range(2):
        both = own_grads[i] + got[i * 4 * BLK : (i + 1) * 4 * BLK]
        low, gain_part = head_backward(both[:, :HD], key_raw[i], key_norm, *rope[i])
        key_gain = key_gain + gain_part
        grad_qkv.append(jnp.concatenate(query_grads[i] + [low, both[:, HD:].astype(BF)], 1))
    grad_normed_one = scatter_tokens(*[times_transposed(g, w_qkv) for g in grad_qkv])
    grad_wqkv = transposed_times(jnp.concatenate(normed_rows), jnp.concatenate(grad_qkv))
    grad_wout = transposed_times(jnp.concatenate(grad_attn), jnp.concatenate(attended))
    gain_one = jnp.sum(grad_wqkv * w_qkv.astype(F32), axis=1) / norm_attn
    attn_grads = jnp.concatenate([grad_wqkv, grad_wout], 1).astype(BF)
    attn_grads = lax.all_to_all(attn_grads, ("yl", "z", "yh"), 0, 0, tiled=True)
    attn_grads = jnp.sum(attn_grads.reshape(16, 64, -1).astype(F32), axis=0).astype(BF)
    attn_grads = swap_shards(attn_grads).astype(F32)

    gains = jnp.concatenate([gain_one, gain_two, query_gain, key_gain]).reshape(18, 128)
    gains = gains + send(gains, c=1)
    for one, two, three in (
        (dict(x=1), dict(x=2), dict(x=3)),
        (dict(z=1), dict(z=2), dict(z=3)),
        (dict(yl=1), dict(yh=1), dict(yl=1, yh=1)),
    ):
        gains = (gains + send(gains, **one)) + (send(gains, **two) + send(gains, **three))
    gains = gains.reshape(-1)

    grad_tokens = grad_middle + rms_backward(grad_normed_one, local_rows, inverse_one, norm_attn)
    return (
        result,
        grad_tokens.astype(BF),
        attn_grads[:, :256],
        attn_grads[:, 256:384],
        attn_grads[:, 384:512],
        attn_grads[:, 512:],
        mlp_grads[:, :384],
        mlp_grads[:, 384:768],
        mlp_grads[:, 768:],
        gains[:1024],
        gains[1024:2048],
        gains[2048:2176],
        gains[2176:],
    )


def solution(mesh):
    whole = Mesh(mesh.devices.reshape(2, 4, 2, 4, 2), AXES)
    dp, tensor = ("yl", "z", "c"), ("x", "yh")
    rows, weight = P(dp + tensor, None), P(dp, tensor)
    in_specs = (rows,) * 2 + (weight,) * 7 + (P(),) * 4 + (P(dp + tensor),) * 2
    out_specs = (rows,) * 2 + (weight,) * 7 + (P(),) * 4
    return jax.shard_map(
        shards, mesh=whole, in_specs=in_specs, out_specs=out_specs, check_vma=False
    )
```

```python
import itertools
import math

import jax
import jax.numpy as jnp
import numpy as np
from jax import lax
from jax.experimental import pallas as pl
from jax.experimental.pallas import tpu as pltpu
from jax.sharding import Mesh
from jax.sharding import PartitionSpec as P

HD = 128
LEN = 1024
BLK = 128

eps_norm = 1e-06
rope_base = 1000000.0
masked_score = -1e30
scale = 1.0 / math.sqrt(HD)

BF = jnp.bfloat16
F32 = jnp.float32

AXES = ("yl", "z", "c", "x", "yh")
SIZES = {"yl": 2, "z": 4, "c": 2, "x": 4, "yh": 2}


def pairs(axes, move):
    sizes = [SIZES[a] for a in axes]
    out = []
    for place in itertools.product(*[range(s) for s in sizes]):
        target = move(dict(zip(axes, place)))
        source = goal = 0
        for a, s, v in zip(axes, sizes, place):
            source = source * s + v
            goal = goal * s + target[a]
        out.append((source, goal))
    return out


def send(value, **flips):
    axes = tuple(a for a in AXES if a in flips)
    table = pairs(axes, lambda p: {a: p[a] ^ flips[a] for a in axes})
    return lax.ppermute(value, axes if len(axes) > 1 else axes[0], table)


def matmul(left, right):
    return jnp.dot(left, right, preferred_element_type=F32)


def times_transposed(left, right):
    return lax.dot_general(left, right, (((1,), (1,)), ((), ())), preferred_element_type=F32)


def transposed_times(left, right):
    return lax.dot_general(left, right, (((0,), (0,)), ((), ())), preferred_element_type=F32)


PAD = 16
ROWS = 4 * BLK
LOG2E = math.log2(math.e)


def call(body, out_shapes, flops=0, copied=()):
    vmem = pl.BlockSpec(memory_space=pltpu.VMEM)
    scratch = [pltpu.VMEM(*c) for c in copied]
    if copied:
        scratch.append(pltpu.SemaphoreType.DMA((len(copied),)))

    def run(scalars, *arrays):
        held = pl.BlockSpec(memory_space=pltpu.HBM) if copied else vmem
        return pl.pallas_call(
            body,
            in_specs=[pl.BlockSpec(memory_space=pltpu.SMEM)] + [held] * len(arrays),
            out_specs=[vmem] * len(out_shapes),
            out_shape=[jax.ShapeDtypeStruct(*o) for o in out_shapes],
            scratch_shapes=scratch,
            compiler_params=pltpu.CompilerParams(vmem_limit_bytes=(60 if copied else 40) << 20),
            cost_estimate=pl.CostEstimate(
                flops=flops,
                bytes_accessed=sum(a.size * a.dtype.itemsize for a in arrays),
                transcendentals=0,
            ),
        )(scalars, *arrays)

    return run


def after(value, *earlier):
    return lax.optimization_barrier((value,) + earlier)[0]


def to_plane(rows):
    groups = [rows[:, i * 128 : (i + 1) * 128] for i in range(8)]
    return jnp.concatenate([g[:, :64] for g in groups] + [g[:, 64:] for g in groups], axis=1)


def from_plane(rows):
    halves = [rows[:, i * 64 : (i + 1) * 64] for i in range(16)]
    return jnp.concatenate([halves[c * 8 + i] for i in range(8) for c in range(2)], axis=1)


def rms_inverse(values):
    return lax.rsqrt(jnp.mean(values * values, axis=-1, keepdims=True) + eps_norm)


def rms_backward(grad_rows, values, inverse, gain):
    scaled = grad_rows * gain
    return inverse * (
        scaled - values * inverse * inverse * jnp.mean(scaled * values, axis=-1, keepdims=True)
    )


def opening(sc, *refs):
    ins, outs, (held, sem) = refs[:12], refs[12:18], (refs[18:30], refs[30])
    copies = [pltpu.make_async_copy(a, b, sem.at[i]) for i, (a, b) in enumerate(zip(ins, held))]
    for copy in copies:
        copy.start()
    for copy in copies:
        copy.wait()
    tokens, cot, gain_one, gain_two, position, wq, wk, wv, wo, wg, wu, wd = held
    o_qkv, o_rest, o_payload, o_tokens, o_cot, o_gains = outs
    o_qkv[:, :256] = wq[...]
    o_qkv[:, 256:384] = wk[...]
    o_qkv[:, 384:] = wv[...]
    o_rest[:, :256] = wo[...]
    o_rest[:, 256:640] = wg[...]
    o_rest[:, 640:1024] = wu[...]
    o_rest[:, 1024:] = wd[...]
    rows = to_plane(tokens[...].astype(F32))
    gain = jnp.concatenate([jnp.broadcast_to(gain_one[...], (4, 1024)),
                            jnp.broadcast_to(gain_two[...], (4, 1024))], 0)
    gain = to_plane(gain)
    o_gains[...] = gain
    o_tokens[...] = rows.astype(BF)
    o_payload[:BLK] = (rows * rms_inverse(rows) * gain[0:1]).astype(BF)
    at = jnp.broadcast_to(position[...], (PAD, BLK))
    first = lax.broadcasted_iota(jnp.int32, (PAD, BLK), 0) == 0
    marks = jnp.where(first, at // 32, at % 32).astype(F32)
    marks = jnp.concatenate([marks, jnp.zeros((PAD, 1024 - BLK), F32)], 1)
    o_payload[BLK:] = marks.astype(BF)
    o_cot[...] = to_plane(cot[...].astype(F32)).astype(BF)


def in_order(sc, arrived, o_rows):
    yl, z, yh = sc[0], sc[1], sc[2]
    for i in range(16):
        slot = ((i % 4) ^ z) * 4 + ((i // 4 % 2) ^ yl) * 2 + ((i // 8) ^ yh)
        o_rows[i * 64 : (i + 1) * 64] = arrived[pl.ds(pl.multiple_of(slot * 64, 64), 64), :]


def roped(rows, cosine, sine):
    return rows * cosine + pltpu.roll(rows, HD // 2, 1) * sine


def unroped(rows, cosine, sine):
    return rows * cosine - pltpu.roll(rows, HD // 2, 1) * sine


def normed_head(part, gain, trig):
    return roped(part * rms_inverse(part) * gain, trig[:, :HD], trig[:, HD:]).astype(BF)


def project_keys(sc, payload, w_qkv, consts, o_rows, o_kv, o_raw, o_trig, o_marks):
    for b in range(4):
        o_rows[b * BLK : (b + 1) * BLK] = payload[b, :BLK]
        marks = payload[b, BLK:, :BLK].astype(F32)
        positions = marks[0:1] * 32.0 + marks[1:2]
        o_marks[:, b * BLK : (b + 1) * BLK] = jnp.broadcast_to(positions, (8, BLK))
        angles = jnp.broadcast_to(positions, (BLK, BLK)).T * consts[2:3]
        o_trig[b * BLK : (b + 1) * BLK, :HD] = jnp.cos(angles)
        o_trig[b * BLK : (b + 1) * BLK, HD:] = jnp.sin(angles) * consts[3:4]
    raw = matmul(o_rows[...], w_qkv[:, 256:])
    o_raw[...] = raw[:, :HD]
    o_kv[:, :HD] = normed_head(raw[:, :HD], consts[1:2], o_trig[...])
    o_kv[:, HD:] = raw[:, HD:].astype(BF)


def project_queries(sc, rows, w_qkv, consts, trig, o_query, o_raw):
    raw = matmul(rows[...], w_qkv[:, :256])
    o_raw[...] = raw
    for h in range(2):
        at = slice(h * HD, (h + 1) * HD)
        o_query[:, at] = normed_head(raw[:, at], consts[0:1], trig[...])


def allowed_keys(sc, far, marks):
    x, yh = sc[3], sc[2]
    lanes = lax.broadcasted_iota(jnp.int32, (8, ROWS), 1)[0:1]
    down = lax.broadcasted_iota(jnp.int32, (ROWS, 128), 0)[:, 0:1]
    query = (2 * (x ^ (lanes // BLK)) + yh) * BLK + lanes % BLK
    key = (2 * (x ^ (down // BLK)) + (1 - yh if far else yh)) * BLK + down % BLK
    first = query - marks[0:1].astype(jnp.int32)
    return (key <= query) & (key >= first)


def expo_scores(key, query, allowed):
    scores = times_transposed(key, query)
    return jnp.where(allowed, jnp.exp2(scores * (scale * LOG2E)), 0.0)


def transposed(rows):
    return rows.astype(F32).T.astype(BF)


def attend_near(sc, query, kv, marks, o_sum, o_total):
    allowed = allowed_keys(sc, False, marks[...])
    value_t = transposed(kv[:, HD:])
    for h in range(2):
        expo = expo_scores(kv[:, :HD], query[:, h * HD : (h + 1) * HD], allowed)
        o_total[h * 8 : h * 8 + 8] = jnp.broadcast_to(jnp.sum(expo, 0, keepdims=True), (8, ROWS))
        o_sum[h * HD : (h + 1) * HD] = matmul(value_t, expo.astype(BF))


def attend_far(sc, query, kv, marks, near_sum, near_total, o_out, o_total):
    allowed = allowed_keys(sc, True, marks[...])
    value_t = transposed(kv[:, HD:])
    for h in range(2):
        expo = expo_scores(kv[:, :HD], query[:, h * HD : (h + 1) * HD], allowed)
        total = near_total[h * 8 : h * 8 + 1] + jnp.sum(expo, 0, keepdims=True)
        o_total[h * 8 : h * 8 + 8] = jnp.broadcast_to(total, (8, ROWS))
        out = near_sum[h * HD : (h + 1) * HD] + matmul(value_t, expo.astype(BF))
        o_out[:, h * HD : (h + 1) * HD] = (out / total).T.astype(BF)


def back_scores(sc, far, query, kv, marks, total, grad, out, o_kv):
    allowed = allowed_keys(sc, far, marks[...])
    key, value = kv[:, :HD], kv[:, HD:]
    key_t = transposed(key)
    key_sum, value_sum, query_grads = 0.0, 0.0, []
    for h in range(2):
        q, g = query[:, h * HD : (h + 1) * HD], grad[:, h * HD : (h + 1) * HD]
        mean = g.astype(F32) * out[:, h * HD : (h + 1) * HD].astype(F32)
        mean = jnp.sum(mean.T, axis=0, keepdims=True)
        weights = expo_scores(key, q, allowed) * (1.0 / total[h * 8 : h * 8 + 1])
        value_sum = value_sum + matmul(weights.astype(BF), g)
        low = (weights * (times_transposed(value, g) - mean) * scale).astype(BF)
        key_sum = key_sum + matmul(low, q)
        query_grads.append(matmul(key_t, low))
    o_kv[:, :HD] = key_sum.astype(o_kv.dtype)
    o_kv[:, HD:] = value_sum.astype(o_kv.dtype)
    return query_grads


def back_far(sc, query, kv, marks, total, grad, out, o_kv, o_query):
    for h, part in enumerate(back_scores(sc, True, query, kv, marks, total, grad, out, o_kv)):
        o_query[h * HD : (h + 1) * HD] = part


def back_near(sc, query, kv, marks, total, grad, out, far_query, raw, trig, consts, o_kv, o_query,
              o_gain):
    parts = back_scores(sc, False, query, kv, marks, total, grad, out, o_kv)
    gain_sum = 0.0
    for h, part in enumerate(parts):
        whole = (part + far_query[h * HD : (h + 1) * HD]).T
        rows = raw[:, h * HD : (h + 1) * HD]
        back = unroped(whole, trig[:, :HD], trig[:, HD:])
        inverse = rms_inverse(rows)
        gain_sum = gain_sum + jnp.sum(back * rows * inverse, axis=0, keepdims=True)
        low = rms_backward(back, rows, inverse, consts[0:1])
        o_query[:, h * HD : (h + 1) * HD] = low.astype(BF)
    o_gain[...] = jnp.broadcast_to(gain_sum, (8, HD))


def back_keys(sc, near, far, query_grad, raw, trig, consts, o_qkv, o_gain):
    both = near[...] + far[...].astype(F32)
    rows = raw[...]
    back = unroped(both[:, :HD], trig[:, :HD], trig[:, HD:])
    inverse = rms_inverse(rows)
    gain_sum = jnp.sum(back * rows * inverse, axis=0, keepdims=True)
    o_gain[...] = jnp.broadcast_to(gain_sum, (8, HD))
    o_qkv[:, :256] = query_grad[...]
    o_qkv[:, 256:384] = rms_backward(back, rows, inverse, consts[1:2]).astype(BF)
    o_qkv[:, 384:] = both[:, HD:].astype(BF)


def core_sum(sc, own, got, o_own, *o_low):
    for k in range(4):
        at = slice(k * BLK, (k + 1) * BLK)
        rows = own[at] + got[at].astype(F32)
        if k:
            o_low[k - 1][...] = rows.astype(BF)
        else:
            o_own[...] = rows


def close_middle(sc, own, one, two, three, tokens, gains, o_middle, o_normed):
    middle = own[...] + one[...].astype(F32) + two[...].astype(F32) + three[...].astype(F32)
    middle = middle + tokens[...].astype(F32)
    o_middle[...] = middle
    o_normed[...] = (middle * rms_inverse(middle) * gains[4:5]).astype(BF)


def close_mlp_grad(sc, own, one, two, three, middle, cot, gains, o_grad, o_low):
    grad = own[...] + one[...].astype(F32) + two[...].astype(F32) + three[...].astype(F32)
    rows = middle[...]
    grad = cot[...].astype(F32) + rms_backward(grad, rows, rms_inverse(rows), gains[4:5])
    o_grad[...] = grad
    o_low[...] = grad.astype(BF)


def close_result(sc, own, one, two, three, middle, o_result):
    rows = own[...] + one[...].astype(F32) + two[...].astype(F32) + three[...].astype(F32)
    o_result[...] = from_plane(rows + middle[...]).astype(BF)


def close_tokens(sc, own, one, two, three, grad_middle, tokens, gains, o_grad):
    grad = own[...] + one[...].astype(F32) + two[...].astype(F32) + three[...].astype(F32)
    rows = tokens[...].astype(F32)
    grad = grad_middle[...] + rms_backward(grad, rows, rms_inverse(rows), gains[0:1])
    o_grad[...] = from_plane(grad).astype(BF)


def gather_tokens(rows):
    got = {k: send(rows, x=k) for k in (2, 1, 3)}
    own = jnp.concatenate([rows, got[1], got[2], got[3]])
    return own, send(own, c=1)


def scatter_tokens(sc, own, other):
    low = [((BLK, 1024), BF)] * 3
    total, *low = call(core_sum, [((BLK, 1024), F32)] + low)(
        sc, own, send(other.astype(BF), c=1)
    )
    got = {k: send(low[k - 1], x=k) for k in (2, 1, 3)}
    return (total, got[1], got[2], got[3]), low[0]


def plane_table(k2, k1):
    return pairs(
        ("yl", "c", "yh"), lambda p: {"c": p["yh"], "yl": p["yl"] ^ k2, "yh": p["c"] ^ k1}
    )


def gather_plane(shard):
    axes = ("yl", "c", "yh")
    got = [lax.ppermute(shard, axes, plane_table(k2, k1)) for k2 in range(2) for k1 in range(2)]
    return jnp.concatenate(got)


PLANE = ("yh", "yl", "z")


def swap_shards(value):
    axes = ("c", "yh")
    return lax.ppermute(value, axes, pairs(axes, lambda p: {"c": p["yh"], "yh": p["c"]}))


def scatter_weights(grads, extra=None):
    blocks = grads.astype(BF).reshape(16, 64, -1)
    if extra is not None:
        more = jnp.broadcast_to(extra.astype(BF)[None], (16,) + extra.shape)
        blocks = jnp.concatenate([blocks, more], 1)
    got = jnp.sum(lax.all_to_all(blocks, PLANE, 0, 0).astype(F32), axis=0)
    own = swap_shards(got[:64].astype(BF)).astype(F32)
    return own if extra is None else (own, got[64:])


def shards(
    tokens,
    cotangent,
    w_query,
    w_key,
    w_value,
    w_output,
    w_gate,
    w_up,
    w_down,
    norm_attn,
    norm_mlp,
    query_norm,
    key_norm,
    segment,
    position,
):
    yl, z, x, yh = (lax.axis_index(a) for a in ("yl", "z", "x", "yh"))
    sc = jnp.stack([yl, z, yh, x]).astype(jnp.int32)

    frequency = rope_base ** (-2.0 * np.arange(HD // 2) / HD)
    sign = np.ones(HD // 2)
    consts = jnp.stack(
        [
            query_norm,
            key_norm,
            jnp.asarray(np.concatenate([frequency, frequency]), F32),
            jnp.asarray(np.concatenate([-sign, sign]), F32),
        ]
    )
    consts = jnp.pad(consts, ((0, 4), (0, 0)))

    given = [tokens, cotangent] + [a.reshape(1, -1) for a in (norm_attn, norm_mlp, position)]
    given += [w_query, w_key, w_value, w_output, w_gate, w_up, w_down]
    qkv_shard, rest_shard, payload, rows_in, cot_in, gains = call(
        opening,
        [
            ((64, 512), BF),
            ((64, 1408), BF),
            ((BLK + PAD, 1024), BF),
            ((BLK, 1024), BF),
            ((BLK, 1024), BF),
            ((8, 1024), F32),
        ],
        copied=[(a.shape, a.dtype) for a in given],
    )(sc, *given)

    plane = gather_plane(qkv_shard)
    whole = {k: send(plane, z=k) for k in (1, 3, 2)}
    got = {k: send(payload, x=k) for k in (2, 1, 3)}
    got[2] = after(got[2], whole[1], whole[3])
    own = jnp.concatenate([payload, got[1], got[2], got[3]])
    gathered = own, send(own, c=1)
    whole = jnp.concatenate([plane, whole[1], whole[2], whole[3]])
    w_qkv = call(in_order, [((1024, 512), BF)])(sc, whole)[0]
    rest = lax.all_gather(swap_shards(rest_shard), PLANE, axis=0, tiled=True)
    w_out, w_gu, w_dn = rest[:, :256], rest[:, 256:1024], rest[:, 1024:]

    keys = [
        call(
            project_keys,
            [
                ((ROWS, 1024), BF),
                ((ROWS, 256), BF),
                ((ROWS, HD), F32),
                ((ROWS, 256), F32),
                ((8, ROWS), F32),
            ],
            flops=2 * ROWS * 1024 * 256,
        )(sc, part.reshape(4, BLK + PAD, 1024), w_qkv, consts)
        for part in gathered
    ]
    normed_rows, near_kv, key_raw, trig, marks = zip(*keys)
    far_kv = send(jnp.concatenate(near_kv), yh=1)
    cot_rows = gather_tokens(after(cot_in, gathered[0]))
    far_kv = [far_kv[:ROWS], far_kv[ROWS:]]
    queries, query_raw = zip(
        *[
            call(
                project_queries,
                [((ROWS, 256), BF), ((ROWS, 256), F32)],
                flops=2 * ROWS * 1024 * 256,
            )(sc, rows, w_qkv, consts, after(t, near_kv[1]))
            for rows, t in zip(normed_rows, trig)
        ]
    )
    near = [
        call(attend_near, [((256, ROWS), F32), ((16, ROWS), F32)], flops=8 * ROWS * ROWS * HD)(
            sc, queries[i], near_kv[i], marks[i]
        )
        for i in range(2)
    ]

    def attend_rest(i, *earlier):
        return call(attend_far, [((ROWS, 256), BF), ((16, ROWS), F32)], flops=8 * ROWS * ROWS * HD)(
            sc, queries[i], after(far_kv[i], *earlier), marks[i], *near[i]
        )

    other = attend_rest(1, near[0][1], cot_rows[0])
    other_part = times_transposed(other[0], w_out)
    own = attend_rest(0, other_part)
    attended = [own, other]
    terms, _ = scatter_tokens(sc, times_transposed(own[0], w_out), other_part)
    middle, normed_two = call(close_middle, [((BLK, 1024), F32), ((BLK, 1024), BF)])(
        sc, *terms, rows_in, gains
    )

    mlp_rows = gather_tokens(normed_two)
    grad_active = [matmul(c, w_dn) for c in cot_rows]
    active, grad_gu = [], []
    for rows, grad in zip(mlp_rows, grad_active):
        gate_up = matmul(rows, w_gu)
        gate, up = gate_up[:, :384], gate_up[:, 384:]
        sigmoid = 1.0 / (1.0 + jnp.exp(-gate))
        silu = gate * sigmoid
        active.append((silu * up).astype(BF))
        grad_gu.append(
            jnp.concatenate(
                [
                    (grad * up * sigmoid * (1.0 + gate * (1.0 - sigmoid))).astype(BF),
                    (grad * silu).astype(BF),
                ],
                axis=1,
            )
        )
    terms, sent = scatter_tokens(sc, *[times_transposed(g, w_gu) for g in grad_gu])
    grad_wgu = sum(transposed_times(r, after(g, sent)) for r, g in zip(mlp_rows, grad_gu))
    grad_wdn = sum(transposed_times(r, after(a, sent)) for r, a in zip(cot_rows, active))
    mlp_blocks = jnp.concatenate([grad_wgu, grad_wdn], 1).astype(BF)
    mlp_grads = lax.psum_scatter(mlp_blocks, PLANE, scatter_dimension=0, tiled=True)
    mlp_grads = swap_shards(mlp_grads).astype(F32)
    grad_middle, grad_low = call(close_mlp_grad, [((BLK, 1024), F32), ((BLK, 1024), BF)])(
        sc, *terms, middle, cot_in, gains
    )
    grad_attn = gather_tokens(grad_low)
    mlp_terms, _ = scatter_tokens(
        sc, *[times_transposed(after(a, grad_attn[0]), w_dn) for a in active]
    )
    result = call(close_result, [((BLK, 1024), BF)])(sc, *mlp_terms, middle)[0]
    gain_two = jnp.sum(grad_wgu * w_gu.astype(F32), axis=1) / gains[4]

    grad_wout = sum(transposed_times(g, a[0]) for g, a in zip(grad_attn, attended))
    grad_attended = [matmul(g, w_out).astype(BF) for g in grad_attn]
    far_back = [
        call(back_far, [((ROWS, 256), BF), ((256, ROWS), F32)], flops=20 * ROWS * ROWS * HD)(
            sc, queries[i], far_kv[i], marks[i], attended[i][1], grad_attended[i], attended[i][0]
        )
        for i in range(2)
    ]
    got = send(jnp.concatenate([b[0] for b in far_back]), yh=1)
    got = [got[:ROWS], got[ROWS:]]
    near_back = [
        call(
            back_near,
            [((ROWS, 256), F32), ((ROWS, 256), BF), ((8, HD), F32)],
            flops=20 * ROWS * ROWS * HD,
        )(
            sc,
            queries[i],
            near_kv[i],
            marks[i],
            attended[i][1],
            grad_attended[i],
            attended[i][0],
            after(far_back[i][1], far_back[1 - i][1]),
            query_raw[i],
            trig[i],
            consts,
        )
        for i in range(2)
    ]
    grad_wq = sum(transposed_times(p, b[1]) for p, b in zip(normed_rows, near_back))

    def close_keys(i, *earlier):
        b = near_back[i]
        return call(back_keys, [((ROWS, 512), BF), ((8, HD), F32)])(
            sc, b[0], after(got[i], *earlier), b[1], key_raw[i], trig[i], consts
        )

    other = close_keys(1, grad_wq, *mlp_terms)
    other_part = times_transposed(other[0], w_qkv)
    own = close_keys(0, other_part)
    final = [own, other]
    terms, sent = scatter_tokens(sc, times_transposed(own[0], w_qkv), other_part)
    grad_tokens = call(close_tokens, [((BLK, 1024), BF)])(
        sc, *terms, grad_middle, rows_in, gains
    )[0]
    grad_wkv = sum(
        transposed_times(p, f[0][:, 256:]) for p, f in zip(normed_rows, final)
    )

    gain_one = jnp.sum(grad_wq * w_qkv[:, :256].astype(F32), axis=1)
    gain_one = (gain_one + jnp.sum(grad_wkv * w_qkv[:, 256:].astype(F32), axis=1)) / gains[0]
    query_gain = sum(b[2][0] for b in near_back)
    key_gain = sum(f[1][0] for f in final)
    sums = jnp.concatenate([gain_one, gain_two, query_gain, key_gain]).reshape(18, 128)
    sums = jnp.pad(sums.reshape(-1), (0, 16 * 768 - 2304)).reshape(16, 768)
    attn_blocks = jnp.concatenate([grad_wq, grad_wkv, grad_wout], 1).astype(BF)
    attn_grads, sums = scatter_weights(
        after(attn_blocks, sent, result), sums + send(sums, c=1)
    )
    sums = sums[:3]
    sums = (sums + send(sums, x=1)) + (send(sums, x=2) + send(sums, x=3))
    sums = sums.reshape(-1)

    def natural(gain):
        return gain.reshape(2, 8, 64).transpose(1, 0, 2).reshape(-1)

    return (
        result,
        grad_tokens,
        attn_grads[:, :256],
        attn_grads[:, 256:384],
        attn_grads[:, 384:512],
        attn_grads[:, 512:],
        mlp_grads[:, :384],
        mlp_grads[:, 384:768],
        mlp_grads[:, 768:],
        natural(sums[:1024]),
        natural(sums[1024:2048]),
        sums[2048:2176],
        sums[2176:2304],
    )


def solution(mesh):
    whole = Mesh(mesh.devices.reshape(2, 4, 2, 4, 2), AXES)
    dp, tensor = ("yl", "z", "c"), ("x", "yh")
    rows, weight = P(dp + tensor, None), P(dp, tensor)
    in_specs = (rows,) * 2 + (weight,) * 7 + (P(),) * 4 + (P(dp + tensor),) * 2
    out_specs = (rows,) * 2 + (weight,) * 7 + (P(),) * 4
    return jax.shard_map(
        shards, mesh=whole, in_specs=in_specs, out_specs=out_specs, check_vma=False
    )
```

```python
import itertools
import math

import jax
import jax.numpy as jnp
import numpy as np
from jax import lax
from jax.experimental import pallas as pl
from jax.experimental.pallas import tpu as pltpu
from jax.sharding import Mesh
from jax.sharding import PartitionSpec as P

HD = 128
LEN = 1024
BLK = 128

eps_norm = 1e-06
rope_base = 1000000.0
masked_score = -1e30
scale = 1.0 / math.sqrt(HD)

BF = jnp.bfloat16
F32 = jnp.float32

AXES = ("yl", "z", "c", "x", "yh")
SIZES = {"yl": 2, "z": 4, "c": 2, "x": 4, "yh": 2}


def pairs(axes, move):
    sizes = [SIZES[a] for a in axes]
    out = []
    for place in itertools.product(*[range(s) for s in sizes]):
        target = move(dict(zip(axes, place)))
        source = goal = 0
        for a, s, v in zip(axes, sizes, place):
            source = source * s + v
            goal = goal * s + target[a]
        out.append((source, goal))
    return out


def send(value, **flips):
    axes = tuple(a for a in AXES if a in flips)
    table = pairs(axes, lambda p: {a: p[a] ^ flips[a] for a in axes})
    return lax.ppermute(value, axes if len(axes) > 1 else axes[0], table)


def matmul(left, right):
    return jnp.dot(left, right, preferred_element_type=F32)


def times_transposed(left, right):
    return lax.dot_general(left, right, (((1,), (1,)), ((), ())), preferred_element_type=F32)


def transposed_times(left, right):
    return lax.dot_general(left, right, (((0,), (0,)), ((), ())), preferred_element_type=F32)


PAD = 16
ROWS = 4 * BLK
LOG2E = math.log2(math.e)


def call(body, out_shapes, flops=0, copied=()):
    vmem = pl.BlockSpec(memory_space=pltpu.VMEM)
    scratch = [pltpu.VMEM(*c) for c in copied]
    if copied:
        scratch.append(pltpu.SemaphoreType.DMA((len(copied),)))

    def run(scalars, *arrays):
        held = pl.BlockSpec(memory_space=pltpu.HBM) if copied else vmem
        return pl.pallas_call(
            body,
            in_specs=[pl.BlockSpec(memory_space=pltpu.SMEM)] + [held] * len(arrays),
            out_specs=[vmem] * len(out_shapes),
            out_shape=[jax.ShapeDtypeStruct(*o) for o in out_shapes],
            scratch_shapes=scratch,
            compiler_params=pltpu.CompilerParams(vmem_limit_bytes=(60 if copied else 40) << 20),
            cost_estimate=pl.CostEstimate(
                flops=flops,
                bytes_accessed=sum(a.size * a.dtype.itemsize for a in arrays),
                transcendentals=0,
            ),
        )(scalars, *arrays)

    return run


def after(value, *earlier):
    return lax.optimization_barrier((value,) + earlier)[0]


def to_plane(rows):
    groups = [rows[:, i * 128 : (i + 1) * 128] for i in range(8)]
    return jnp.concatenate([g[:, :64] for g in groups] + [g[:, 64:] for g in groups], axis=1)


def from_plane(rows):
    halves = [rows[:, i * 64 : (i + 1) * 64] for i in range(16)]
    return jnp.concatenate([halves[c * 8 + i] for i in range(8) for c in range(2)], axis=1)


def rms_inverse(values):
    return lax.rsqrt(jnp.mean(values * values, axis=-1, keepdims=True) + eps_norm)


def rms_backward(grad_rows, values, inverse, gain):
    scaled = grad_rows * gain
    return inverse * (
        scaled - values * inverse * inverse * jnp.mean(scaled * values, axis=-1, keepdims=True)
    )


def opening(sc, *refs):
    ins, outs, (held, sem) = refs[:12], refs[12:18], (refs[18:30], refs[30])
    copies = [pltpu.make_async_copy(a, b, sem.at[i]) for i, (a, b) in enumerate(zip(ins, held))]
    for copy in copies:
        copy.start()
    for copy in copies:
        copy.wait()
    tokens, cot, gain_one, gain_two, position, wq, wk, wv, wo, wg, wu, wd = held
    o_qkv, o_rest, o_payload, o_tokens, o_cot, o_gains = outs
    o_qkv[:, :256] = wq[...]
    o_qkv[:, 256:384] = wk[...]
    o_qkv[:, 384:] = wv[...]
    o_rest[:, :256] = wo[...]
    o_rest[:, 256:640] = wg[...]
    o_rest[:, 640:1024] = wu[...]
    o_rest[:, 1024:] = wd[...]
    rows = to_plane(tokens[...].astype(F32))
    gain = jnp.concatenate([jnp.broadcast_to(gain_one[...], (4, 1024)),
                            jnp.broadcast_to(gain_two[...], (4, 1024))], 0)
    gain = to_plane(gain)
    o_gains[...] = gain
    o_tokens[...] = rows.astype(BF)
    o_payload[:BLK] = (rows * rms_inverse(rows) * gain[0:1]).astype(BF)
    at = jnp.broadcast_to(position[...], (PAD, BLK))
    first = lax.broadcasted_iota(jnp.int32, (PAD, BLK), 0) == 0
    marks = jnp.where(first, at // 32, at % 32).astype(F32)
    marks = jnp.concatenate([marks, jnp.zeros((PAD, 1024 - BLK), F32)], 1)
    o_payload[BLK:] = marks.astype(BF)
    o_cot[...] = to_plane(cot[...].astype(F32)).astype(BF)


def in_order(sc, arrived, o_rows):
    yl, z, yh = sc[0], sc[1], sc[2]
    for i in range(16):
        slot = ((i % 4) ^ z) * 4 + ((i // 4 % 2) ^ yl) * 2 + ((i // 8) ^ yh)
        o_rows[i * 64 : (i + 1) * 64] = arrived[pl.ds(pl.multiple_of(slot * 64, 64), 64), :]


def roped(rows, cosine, sine):
    return rows * cosine + pltpu.roll(rows, HD // 2, 1) * sine


def unroped(rows, cosine, sine):
    return rows * cosine - pltpu.roll(rows, HD // 2, 1) * sine


def normed_head(part, gain, trig):
    return roped(part * rms_inverse(part) * gain, trig[:, :HD], trig[:, HD:]).astype(BF)


def project_keys(sc, payload, w_qkv, consts, o_rows, o_kv, o_raw, o_trig, o_marks):
    for b in range(4):
        o_rows[b * BLK : (b + 1) * BLK] = payload[b, :BLK]
        marks = payload[b, BLK:, :BLK].astype(F32)
        positions = marks[0:1] * 32.0 + marks[1:2]
        o_marks[:, b * BLK : (b + 1) * BLK] = jnp.broadcast_to(positions, (8, BLK))
        angles = jnp.broadcast_to(positions, (BLK, BLK)).T * consts[2:3]
        o_trig[b * BLK : (b + 1) * BLK, :HD] = jnp.cos(angles)
        o_trig[b * BLK : (b + 1) * BLK, HD:] = jnp.sin(angles) * consts[3:4]
    raw = matmul(o_rows[...], w_qkv[:, 256:])
    o_raw[...] = raw[:, :HD]
    o_kv[:, :HD] = normed_head(raw[:, :HD], consts[1:2], o_trig[...])
    o_kv[:, HD:] = raw[:, HD:].astype(BF)


def project_queries(sc, rows, w_qkv, consts, trig, o_query, o_raw):
    raw = matmul(rows[...], w_qkv[:, :256])
    o_raw[...] = raw
    for h in range(2):
        at = slice(h * HD, (h + 1) * HD)
        o_query[:, at] = normed_head(raw[:, at], consts[0:1], trig[...])


def allowed_keys(sc, far, marks):
    x, yh = sc[3], sc[2]
    lanes = lax.broadcasted_iota(jnp.int32, (8, ROWS), 1)[0:1]
    down = lax.broadcasted_iota(jnp.int32, (ROWS, 128), 0)[:, 0:1]
    query = (2 * (x ^ (lanes // BLK)) + yh) * BLK + lanes % BLK
    key = (2 * (x ^ (down // BLK)) + (1 - yh if far else yh)) * BLK + down % BLK
    first = query - marks[0:1].astype(jnp.int32)
    return (key <= query) & (key >= first)


def expo_scores(key, query, allowed):
    scores = times_transposed(key, query)
    return jnp.where(allowed, jnp.exp2(scores * (scale * LOG2E)), 0.0)


def transposed(rows):
    return rows.astype(F32).T.astype(BF)


def attend_near(sc, query, kv, marks, o_sum, o_total):
    allowed = allowed_keys(sc, False, marks[...])
    value_t = transposed(kv[:, HD:])
    for h in range(2):
        expo = expo_scores(kv[:, :HD], query[:, h * HD : (h + 1) * HD], allowed)
        o_total[h * 8 : h * 8 + 8] = jnp.broadcast_to(jnp.sum(expo, 0, keepdims=True), (8, ROWS))
        o_sum[h * HD : (h + 1) * HD] = matmul(value_t, expo.astype(BF))


def attend_far(sc, query, kv, marks, near_sum, near_total, o_out, o_total):
    allowed = allowed_keys(sc, True, marks[...])
    value_t = transposed(kv[:, HD:])
    for h in range(2):
        expo = expo_scores(kv[:, :HD], query[:, h * HD : (h + 1) * HD], allowed)
        total = near_total[h * 8 : h * 8 + 1] + jnp.sum(expo, 0, keepdims=True)
        o_total[h * 8 : h * 8 + 8] = jnp.broadcast_to(total, (8, ROWS))
        out = near_sum[h * HD : (h + 1) * HD] + matmul(value_t, expo.astype(BF))
        o_out[:, h * HD : (h + 1) * HD] = (out / total).T.astype(BF)


def back_scores(sc, far, query, kv, marks, total, grad, out, o_kv):
    allowed = allowed_keys(sc, far, marks[...])
    key, value = kv[:, :HD], kv[:, HD:]
    key_t = transposed(key)
    key_sum, value_sum, query_grads = 0.0, 0.0, []
    for h in range(2):
        q, g = query[:, h * HD : (h + 1) * HD], grad[:, h * HD : (h + 1) * HD]
        mean = g.astype(F32) * out[:, h * HD : (h + 1) * HD].astype(F32)
        mean = jnp.sum(mean.T, axis=0, keepdims=True)
        weights = expo_scores(key, q, allowed) * (1.0 / total[h * 8 : h * 8 + 1])
        value_sum = value_sum + matmul(weights.astype(BF), g)
        low = (weights * (times_transposed(value, g) - mean) * scale).astype(BF)
        key_sum = key_sum + matmul(low, q)
        query_grads.append(matmul(key_t, low))
    o_kv[:, :HD] = key_sum.astype(o_kv.dtype)
    o_kv[:, HD:] = value_sum.astype(o_kv.dtype)
    return query_grads


def back_far(sc, query, kv, marks, total, grad, out, o_kv, o_query):
    for h, part in enumerate(back_scores(sc, True, query, kv, marks, total, grad, out, o_kv)):
        o_query[h * HD : (h + 1) * HD] = part


def back_near(sc, query, kv, marks, total, grad, out, far_query, raw, trig, consts, o_kv, o_query,
              o_gain):
    parts = back_scores(sc, False, query, kv, marks, total, grad, out, o_kv)
    gain_sum = 0.0
    for h, part in enumerate(parts):
        whole = (part + far_query[h * HD : (h + 1) * HD]).T
        rows = raw[:, h * HD : (h + 1) * HD]
        back = unroped(whole, trig[:, :HD], trig[:, HD:])
        inverse = rms_inverse(rows)
        gain_sum = gain_sum + jnp.sum(back * rows * inverse, axis=0, keepdims=True)
        low = rms_backward(back, rows, inverse, consts[0:1])
        o_query[:, h * HD : (h + 1) * HD] = low.astype(BF)
    o_gain[...] = jnp.broadcast_to(gain_sum, (8, HD))


def back_keys(sc, near, far, query_grad, raw, trig, consts, o_qkv, o_gain):
    both = near[...] + far[...].astype(F32)
    rows = raw[...]
    back = unroped(both[:, :HD], trig[:, :HD], trig[:, HD:])
    inverse = rms_inverse(rows)
    gain_sum = jnp.sum(back * rows * inverse, axis=0, keepdims=True)
    o_gain[...] = jnp.broadcast_to(gain_sum, (8, HD))
    o_qkv[:, :256] = query_grad[...]
    o_qkv[:, 256:384] = rms_backward(back, rows, inverse, consts[1:2]).astype(BF)
    o_qkv[:, 384:] = both[:, HD:].astype(BF)


def core_sum(sc, own, got, o_own, *o_low):
    for k in range(4):
        at = slice(k * BLK, (k + 1) * BLK)
        rows = own[at] + got[at].astype(F32)
        if k:
            o_low[k - 1][...] = rows.astype(BF)
        else:
            o_own[...] = rows


def close_middle(sc, own, one, two, three, tokens, gains, o_middle, o_normed):
    middle = own[...] + one[...].astype(F32) + two[...].astype(F32) + three[...].astype(F32)
    middle = middle + tokens[...].astype(F32)
    o_middle[...] = middle
    o_normed[...] = (middle * rms_inverse(middle) * gains[4:5]).astype(BF)


def close_mlp_grad(sc, own, one, two, three, middle, cot, gains, o_grad, o_low):
    grad = own[...] + one[...].astype(F32) + two[...].astype(F32) + three[...].astype(F32)
    rows = middle[...]
    grad = cot[...].astype(F32) + rms_backward(grad, rows, rms_inverse(rows), gains[4:5])
    o_grad[...] = grad
    o_low[...] = grad.astype(BF)


def close_result(sc, own, one, two, three, middle, o_result):
    rows = own[...] + one[...].astype(F32) + two[...].astype(F32) + three[...].astype(F32)
    o_result[...] = from_plane(rows + middle[...]).astype(BF)


def close_tokens(sc, own, one, two, three, grad_middle, tokens, gains, o_grad):
    grad = own[...] + one[...].astype(F32) + two[...].astype(F32) + three[...].astype(F32)
    rows = tokens[...].astype(F32)
    grad = grad_middle[...] + rms_backward(grad, rows, rms_inverse(rows), gains[0:1])
    o_grad[...] = from_plane(grad).astype(BF)


def gather_tokens(rows):
    got = {k: send(rows, x=k) for k in (2, 1, 3)}
    own = jnp.concatenate([rows, got[1], got[2], got[3]])
    return own, send(own, c=1)


def scatter_tokens(sc, own, other):
    low = [((BLK, 1024), BF)] * 3
    total, *low = call(core_sum, [((BLK, 1024), F32)] + low)(
        sc, own, send(other.astype(BF), c=1)
    )
    got = {k: send(low[k - 1], x=k) for k in (2, 1, 3)}
    return (total, got[1], got[2], got[3]), low[0]


def plane_table(k2, k1):
    return pairs(
        ("yl", "c", "yh"), lambda p: {"c": p["yh"], "yl": p["yl"] ^ k2, "yh": p["c"] ^ k1}
    )


def gather_plane(shard):
    axes = ("yl", "c", "yh")
    got = [lax.ppermute(shard, axes, plane_table(k2, k1)) for k2 in range(2) for k1 in range(2)]
    return jnp.concatenate(got)


PLANE = ("yh", "yl", "z")


def swap_shards(value):
    axes = ("c", "yh")
    return lax.ppermute(value, axes, pairs(axes, lambda p: {"c": p["yh"], "yh": p["c"]}))


def scatter_weights(grads, extra=None):
    blocks = grads.astype(BF).reshape(16, 64, -1)
    if extra is not None:
        more = jnp.broadcast_to(extra.astype(BF)[None], (16,) + extra.shape)
        blocks = jnp.concatenate([blocks, more], 1)
    got = jnp.sum(lax.all_to_all(blocks, PLANE, 0, 0).astype(F32), axis=0)
    own = swap_shards(got[:64].astype(BF)).astype(F32)
    return own if extra is None else (own, got[64:])


def shards(
    tokens,
    cotangent,
    w_query,
    w_key,
    w_value,
    w_output,
    w_gate,
    w_up,
    w_down,
    norm_attn,
    norm_mlp,
    query_norm,
    key_norm,
    segment,
    position,
):
    yl, z, x, yh = (lax.axis_index(a) for a in ("yl", "z", "x", "yh"))
    sc = jnp.stack([yl, z, yh, x]).astype(jnp.int32)

    frequency = rope_base ** (-2.0 * np.arange(HD // 2) / HD)
    sign = np.ones(HD // 2)
    consts = jnp.stack(
        [
            query_norm,
            key_norm,
            jnp.asarray(np.concatenate([frequency, frequency]), F32),
            jnp.asarray(np.concatenate([-sign, sign]), F32),
        ]
    )
    consts = jnp.pad(consts, ((0, 4), (0, 0)))

    given = [tokens, cotangent] + [a.reshape(1, -1) for a in (norm_attn, norm_mlp, position)]
    given += [w_query, w_key, w_value, w_output, w_gate, w_up, w_down]
    qkv_shard, rest_shard, payload, rows_in, cot_in, gains = call(
        opening,
        [
            ((64, 512), BF),
            ((64, 1408), BF),
            ((BLK + PAD, 1024), BF),
            ((BLK, 1024), BF),
            ((BLK, 1024), BF),
            ((8, 1024), F32),
        ],
        copied=[(a.shape, a.dtype) for a in given],
    )(sc, *given)

    plane = gather_plane(qkv_shard)
    whole = {k: send(plane, z=k) for k in (1, 3, 2)}
    got = {k: send(payload, x=k) for k in (2, 1, 3)}
    got[2] = after(got[2], whole[1], whole[3])
    own = jnp.concatenate([payload, got[1], got[2], got[3]])
    gathered = own, send(own, c=1)
    whole = jnp.concatenate([plane, whole[1], whole[2], whole[3]])
    w_qkv = call(in_order, [((1024, 512), BF)])(sc, whole)[0]
    rest = lax.all_gather(swap_shards(rest_shard), PLANE, axis=0, tiled=True)
    w_out, w_gu, w_dn = rest[:, :256], rest[:, 256:1024], rest[:, 1024:]

    keys = [
        call(
            project_keys,
            [
                ((ROWS, 1024), BF),
                ((ROWS, 256), BF),
                ((ROWS, HD), F32),
                ((ROWS, 256), F32),
                ((8, ROWS), F32),
            ],
            flops=2 * ROWS * 1024 * 256,
        )(sc, part.reshape(4, BLK + PAD, 1024), w_qkv, consts)
        for part in gathered
    ]
    normed_rows, near_kv, key_raw, trig, marks = zip(*keys)
    far_kv = send(jnp.concatenate(near_kv), yh=1)
    cot_rows = gather_tokens(after(cot_in, gathered[0]))
    far_kv = [far_kv[:ROWS], far_kv[ROWS:]]
    queries, query_raw = zip(
        *[
            call(
                project_queries,
                [((ROWS, 256), BF), ((ROWS, 256), F32)],
                flops=2 * ROWS * 1024 * 256,
            )(sc, rows, w_qkv, consts, after(t, near_kv[1]))
            for rows, t in zip(normed_rows, trig)
        ]
    )
    near = [
        call(attend_near, [((256, ROWS), F32), ((16, ROWS), F32)], flops=8 * ROWS * ROWS * HD)(
            sc, queries[i], near_kv[i], marks[i]
        )
        for i in range(2)
    ]

    def attend_rest(i, *earlier):
        return call(attend_far, [((ROWS, 256), BF), ((16, ROWS), F32)], flops=8 * ROWS * ROWS * HD)(
            sc, queries[i], after(far_kv[i], *earlier), marks[i], *near[i]
        )

    other = attend_rest(1, near[0][1], cot_rows[0])
    other_part = times_transposed(other[0], w_out)
    own = attend_rest(0, other_part)
    attended = [own, other]
    terms, _ = scatter_tokens(sc, times_transposed(own[0], w_out), other_part)
    middle, normed_two = call(close_middle, [((BLK, 1024), F32), ((BLK, 1024), BF)])(
        sc, *terms, rows_in, gains
    )

    mlp_rows = gather_tokens(normed_two)
    grad_active = [matmul(c, w_dn) for c in cot_rows]
    active, grad_gu = [], []
    for rows, grad in zip(mlp_rows, grad_active):
        gate_up = matmul(rows, w_gu)
        gate, up = gate_up[:, :384], gate_up[:, 384:]
        sigmoid = 1.0 / (1.0 + jnp.exp(-gate))
        silu = gate * sigmoid
        active.append((silu * up).astype(BF))
        grad_gu.append(
            jnp.concatenate(
                [
                    (grad * up * sigmoid * (1.0 + gate * (1.0 - sigmoid))).astype(BF),
                    (grad * silu).astype(BF),
                ],
                axis=1,
            )
        )
    terms, sent = scatter_tokens(sc, *[times_transposed(g, w_gu) for g in grad_gu])
    grad_wgu = sum(transposed_times(r, after(g, sent)) for r, g in zip(mlp_rows, grad_gu))
    grad_wdn = sum(transposed_times(r, after(a, sent)) for r, a in zip(cot_rows, active))
    mlp_blocks = jnp.concatenate([grad_wgu, grad_wdn], 1).astype(BF)
    mlp_sum = lax.all_to_all(mlp_blocks.reshape(16, 64, 1152), PLANE, 0, 0)
    mlp_sum = jnp.sum(mlp_sum.astype(F32), axis=0)
    mlp_grads = mlp_sum.astype(BF)
    mlp_grads = swap_shards(mlp_grads).astype(F32)
    grad_middle, grad_low = call(close_mlp_grad, [((BLK, 1024), F32), ((BLK, 1024), BF)])(
        sc, *terms, middle, cot_in, gains
    )
    grad_attn = gather_tokens(grad_low)
    mlp_terms, _ = scatter_tokens(
        sc, *[times_transposed(after(a, grad_attn[0]), w_dn) for a in active]
    )
    result = call(close_result, [((BLK, 1024), BF)])(sc, *mlp_terms, middle)[0]
    gain_two = jnp.sum(grad_wgu * w_gu.astype(F32), axis=1) / gains[4]

    grad_wout = sum(transposed_times(g, a[0]) for g, a in zip(grad_attn, attended))
    grad_attended = [matmul(g, w_out).astype(BF) for g in grad_attn]
    far_back = [
        call(back_far, [((ROWS, 256), BF), ((256, ROWS), F32)], flops=20 * ROWS * ROWS * HD)(
            sc, queries[i], far_kv[i], marks[i], attended[i][1], grad_attended[i], attended[i][0]
        )
        for i in range(2)
    ]
    got = send(jnp.concatenate([b[0] for b in far_back]), yh=1)
    got = [got[:ROWS], got[ROWS:]]
    near_back = [
        call(
            back_near,
            [((ROWS, 256), F32), ((ROWS, 256), BF), ((8, HD), F32)],
            flops=20 * ROWS * ROWS * HD,
        )(
            sc,
            queries[i],
            near_kv[i],
            marks[i],
            attended[i][1],
            grad_attended[i],
            attended[i][0],
            after(far_back[i][1], far_back[1 - i][1], mlp_sum),
            query_raw[i],
            trig[i],
            consts,
        )
        for i in range(2)
    ]
    grad_wq = sum(transposed_times(p, b[1]) for p, b in zip(normed_rows, near_back))

    def close_keys(i, *earlier):
        b = near_back[i]
        return call(back_keys, [((ROWS, 512), BF), ((8, HD), F32)])(
            sc, b[0], after(got[i], *earlier), b[1], key_raw[i], trig[i], consts
        )

    other = close_keys(1, grad_wq, *mlp_terms)
    other_part = times_transposed(other[0], w_qkv)
    own = close_keys(0, other_part)
    final = [own, other]
    terms, sent = scatter_tokens(sc, times_transposed(own[0], w_qkv), other_part)
    grad_tokens = call(close_tokens, [((BLK, 1024), BF)])(
        sc, *terms, grad_middle, rows_in, gains
    )[0]
    grad_wkv = sum(
        transposed_times(p, f[0][:, 256:]) for p, f in zip(normed_rows, final)
    )

    gain_one = jnp.sum(grad_wq * w_qkv[:, :256].astype(F32), axis=1)
    gain_one = (gain_one + jnp.sum(grad_wkv * w_qkv[:, 256:].astype(F32), axis=1)) / gains[0]
    query_gain = sum(b[2][0] for b in near_back)
    key_gain = sum(f[1][0] for f in final)
    sums = jnp.concatenate([gain_one, gain_two, query_gain, key_gain]).reshape(18, 128)
    sums = jnp.pad(sums.reshape(-1), (0, 16 * 768 - 2304)).reshape(16, 768)
    attn_blocks = jnp.concatenate([grad_wq, grad_wkv, grad_wout], 1).astype(BF)
    attn_grads, sums = scatter_weights(
        after(attn_blocks, sent, result), sums + send(sums, c=1)
    )
    sums = sums[:3]
    sums = (sums + send(sums, x=1)) + (send(sums, x=2) + send(sums, x=3))
    sums = sums.reshape(-1)

    def natural(gain):
        return gain.reshape(2, 8, 64).transpose(1, 0, 2).reshape(-1)

    return (
        result,
        grad_tokens,
        attn_grads[:, :256],
        attn_grads[:, 256:384],
        attn_grads[:, 384:512],
        attn_grads[:, 512:],
        mlp_grads[:, :384],
        mlp_grads[:, 384:768],
        mlp_grads[:, 768:],
        natural(sums[:1024]),
        natural(sums[1024:2048]),
        sums[2048:2176],
        sums[2176:2304],
    )


def solution(mesh):
    whole = Mesh(mesh.devices.reshape(2, 4, 2, 4, 2), AXES)
    dp, tensor = ("yl", "z", "c"), ("x", "yh")
    rows, weight = P(dp + tensor, None), P(dp, tensor)
    in_specs = (rows,) * 2 + (weight,) * 7 + (P(),) * 4 + (P(dp + tensor),) * 2
    out_specs = (rows,) * 2 + (weight,) * 7 + (P(),) * 4
    return jax.shard_map(
        shards, mesh=whole, in_specs=in_specs, out_specs=out_specs, check_vma=False
    )
```

```python
import itertools
import math

import jax
import jax.numpy as jnp
import numpy as np
from jax import lax
from jax.experimental import pallas as pl
from jax.experimental.pallas import tpu as pltpu
from jax.sharding import Mesh
from jax.sharding import PartitionSpec as P

HD = 128
LEN = 1024
BLK = 128

eps_norm = 1e-06
rope_base = 1000000.0
masked_score = -1e30
scale = 1.0 / math.sqrt(HD)

BF = jnp.bfloat16
F32 = jnp.float32

AXES = ("yl", "z", "c", "x", "yh")
SIZES = {"yl": 2, "z": 4, "c": 2, "x": 4, "yh": 2}


def pairs(axes, move):
    sizes = [SIZES[a] for a in axes]
    out = []
    for place in itertools.product(*[range(s) for s in sizes]):
        target = move(dict(zip(axes, place)))
        source = goal = 0
        for a, s, v in zip(axes, sizes, place):
            source = source * s + v
            goal = goal * s + target[a]
        out.append((source, goal))
    return out


def send(value, **flips):
    axes = tuple(a for a in AXES if a in flips)
    table = pairs(axes, lambda p: {a: p[a] ^ flips[a] for a in axes})
    return lax.ppermute(value, axes if len(axes) > 1 else axes[0], table)


def matmul(left, right):
    return jnp.dot(left, right, preferred_element_type=F32)


def times_transposed(left, right):
    return lax.dot_general(left, right, (((1,), (1,)), ((), ())), preferred_element_type=F32)


def transposed_times(left, right):
    return lax.dot_general(left, right, (((0,), (0,)), ((), ())), preferred_element_type=F32)


PAD = 16
ROWS = 4 * BLK
LOG2E = math.log2(math.e)


def call(body, out_shapes, flops=0, copied=()):
    vmem = pl.BlockSpec(memory_space=pltpu.VMEM)
    scratch = [pltpu.VMEM(*c) for c in copied]
    if copied:
        scratch.append(pltpu.SemaphoreType.DMA((len(copied),)))

    def run(scalars, *arrays):
        held = pl.BlockSpec(memory_space=pltpu.HBM) if copied else vmem
        return pl.pallas_call(
            body,
            in_specs=[pl.BlockSpec(memory_space=pltpu.SMEM)] + [held] * len(arrays),
            out_specs=[vmem] * len(out_shapes),
            out_shape=[jax.ShapeDtypeStruct(*o) for o in out_shapes],
            scratch_shapes=scratch,
            compiler_params=pltpu.CompilerParams(vmem_limit_bytes=(60 if copied else 40) << 20),
            cost_estimate=pl.CostEstimate(
                flops=flops,
                bytes_accessed=sum(a.size * a.dtype.itemsize for a in arrays),
                transcendentals=0,
            ),
        )(scalars, *arrays)

    return run


def after(value, *earlier):
    return lax.optimization_barrier((value,) + earlier)[0]


def to_plane(rows):
    groups = [rows[:, i * 128 : (i + 1) * 128] for i in range(8)]
    return jnp.concatenate([g[:, :64] for g in groups] + [g[:, 64:] for g in groups], axis=1)


def from_plane(rows):
    halves = [rows[:, i * 64 : (i + 1) * 64] for i in range(16)]
    return jnp.concatenate([halves[c * 8 + i] for i in range(8) for c in range(2)], axis=1)


def rms_inverse(values):
    return lax.rsqrt(jnp.mean(values * values, axis=-1, keepdims=True) + eps_norm)


def rms_backward(grad_rows, values, inverse, gain):
    scaled = grad_rows * gain
    return inverse * (
        scaled - values * inverse * inverse * jnp.mean(scaled * values, axis=-1, keepdims=True)
    )


def opening(sc, *refs):
    ins, outs, (held, sem) = refs[:12], refs[12:18], (refs[18:30], refs[30])
    copies = [pltpu.make_async_copy(a, b, sem.at[i]) for i, (a, b) in enumerate(zip(ins, held))]
    for copy in copies:
        copy.start()
    for copy in copies:
        copy.wait()
    tokens, cot, gain_one, gain_two, position, wq, wk, wv, wo, wg, wu, wd = held
    o_qkv, o_rest, o_payload, o_tokens, o_cot, o_gains = outs
    o_qkv[:, :256] = wq[...]
    o_qkv[:, 256:384] = wk[...]
    o_qkv[:, 384:] = wv[...]
    o_rest[:, :256] = wo[...]
    o_rest[:, 256:640] = wg[...]
    o_rest[:, 640:1024] = wu[...]
    o_rest[:, 1024:] = wd[...]
    rows = to_plane(tokens[...].astype(F32))
    gain = jnp.concatenate([jnp.broadcast_to(gain_one[...], (4, 1024)),
                            jnp.broadcast_to(gain_two[...], (4, 1024))], 0)
    gain = to_plane(gain)
    o_gains[...] = gain
    o_tokens[...] = rows.astype(BF)
    o_payload[:BLK] = (rows * rms_inverse(rows) * gain[0:1]).astype(BF)
    at = jnp.broadcast_to(position[...], (PAD, BLK))
    first = lax.broadcasted_iota(jnp.int32, (PAD, BLK), 0) == 0
    marks = jnp.where(first, at // 32, at % 32).astype(F32)
    marks = jnp.concatenate([marks, jnp.zeros((PAD, 1024 - BLK), F32)], 1)
    o_payload[BLK:] = marks.astype(BF)
    o_cot[...] = to_plane(cot[...].astype(F32)).astype(BF)


def in_order(sc, arrived, o_rows):
    yl, z, yh = sc[0], sc[1], sc[2]
    for i in range(16):
        slot = ((i % 4) ^ z) * 4 + ((i // 4 % 2) ^ yl) * 2 + ((i // 8) ^ yh)
        o_rows[i * 64 : (i + 1) * 64] = arrived[pl.ds(pl.multiple_of(slot * 64, 64), 64), :]


def roped(rows, cosine, sine):
    return rows * cosine + pltpu.roll(rows, HD // 2, 1) * sine


def unroped(rows, cosine, sine):
    return rows * cosine - pltpu.roll(rows, HD // 2, 1) * sine


def normed_head(part, gain, trig):
    return roped(part * rms_inverse(part) * gain, trig[:, :HD], trig[:, HD:]).astype(BF)


def project_keys(sc, payload, w_qkv, consts, o_rows, o_kv, o_raw, o_trig, o_marks):
    for b in range(4):
        o_rows[b * BLK : (b + 1) * BLK] = payload[b, :BLK]
        marks = payload[b, BLK:, :BLK].astype(F32)
        positions = marks[0:1] * 32.0 + marks[1:2]
        o_marks[:, b * BLK : (b + 1) * BLK] = jnp.broadcast_to(positions, (8, BLK))
        angles = jnp.broadcast_to(positions, (BLK, BLK)).T * consts[2:3]
        o_trig[b * BLK : (b + 1) * BLK, :HD] = jnp.cos(angles)
        o_trig[b * BLK : (b + 1) * BLK, HD:] = jnp.sin(angles) * consts[3:4]
    raw = matmul(o_rows[...], w_qkv[:, 256:])
    o_raw[...] = raw[:, :HD]
    o_kv[:, :HD] = normed_head(raw[:, :HD], consts[1:2], o_trig[...])
    o_kv[:, HD:] = raw[:, HD:].astype(BF)


def project_queries(sc, rows, w_qkv, consts, trig, o_query, o_raw):
    raw = matmul(rows[...], w_qkv[:, :256])
    o_raw[...] = raw
    for h in range(2):
        at = slice(h * HD, (h + 1) * HD)
        o_query[:, at] = normed_head(raw[:, at], consts[0:1], trig[...])


def allowed_keys(sc, far, marks):
    x, yh = sc[3], sc[2]
    lanes = lax.broadcasted_iota(jnp.int32, (8, ROWS), 1)[0:1]
    down = lax.broadcasted_iota(jnp.int32, (ROWS, 128), 0)[:, 0:1]
    query = (2 * (x ^ (lanes // BLK)) + yh) * BLK + lanes % BLK
    key = (2 * (x ^ (down // BLK)) + (1 - yh if far else yh)) * BLK + down % BLK
    first = query - marks[0:1].astype(jnp.int32)
    return (key <= query) & (key >= first)


def expo_scores(key, query, allowed):
    scores = times_transposed(key, query)
    return jnp.where(allowed, jnp.exp2(scores * (scale * LOG2E)), 0.0)


def transposed(rows):
    return rows.astype(F32).T.astype(BF)


def attend_near(sc, query, kv, marks, o_sum, o_total):
    allowed = allowed_keys(sc, False, marks[...])
    value_t = transposed(kv[:, HD:])
    for h in range(2):
        expo = expo_scores(kv[:, :HD], query[:, h * HD : (h + 1) * HD], allowed)
        o_total[h * 8 : h * 8 + 8] = jnp.broadcast_to(jnp.sum(expo, 0, keepdims=True), (8, ROWS))
        o_sum[h * HD : (h + 1) * HD] = matmul(value_t, expo.astype(BF))


def attend_far(sc, query, kv, marks, near_sum, near_total, o_out, o_total):
    allowed = allowed_keys(sc, True, marks[...])
    value_t = transposed(kv[:, HD:])
    for h in range(2):
        expo = expo_scores(kv[:, :HD], query[:, h * HD : (h + 1) * HD], allowed)
        total = near_total[h * 8 : h * 8 + 1] + jnp.sum(expo, 0, keepdims=True)
        o_total[h * 8 : h * 8 + 8] = jnp.broadcast_to(total, (8, ROWS))
        out = near_sum[h * HD : (h + 1) * HD] + matmul(value_t, expo.astype(BF))
        o_out[:, h * HD : (h + 1) * HD] = (out / total).T.astype(BF)


def back_scores(sc, far, query, kv, marks, total, grad, out, o_kv):
    allowed = allowed_keys(sc, far, marks[...])
    key, value = kv[:, :HD], kv[:, HD:]
    key_t = transposed(key)
    key_sum, value_sum, query_grads = 0.0, 0.0, []
    for h in range(2):
        q, g = query[:, h * HD : (h + 1) * HD], grad[:, h * HD : (h + 1) * HD]
        mean = g.astype(F32) * out[:, h * HD : (h + 1) * HD].astype(F32)
        mean = jnp.sum(mean.T, axis=0, keepdims=True)
        weights = expo_scores(key, q, allowed) * (1.0 / total[h * 8 : h * 8 + 1])
        value_sum = value_sum + matmul(weights.astype(BF), g)
        low = (weights * (times_transposed(value, g) - mean) * scale).astype(BF)
        key_sum = key_sum + matmul(low, q)
        query_grads.append(matmul(key_t, low))
    o_kv[:, :HD] = key_sum.astype(o_kv.dtype)
    o_kv[:, HD:] = value_sum.astype(o_kv.dtype)
    return query_grads


def back_far(sc, query, kv, marks, total, grad, out, o_kv, o_query):
    for h, part in enumerate(back_scores(sc, True, query, kv, marks, total, grad, out, o_kv)):
        o_query[h * HD : (h + 1) * HD] = part


def back_near(sc, query, kv, marks, total, grad, out, far_query, raw, trig, consts, o_kv, o_query,
              o_gain):
    parts = back_scores(sc, False, query, kv, marks, total, grad, out, o_kv)
    gain_sum = 0.0
    for h, part in enumerate(parts):
        whole = (part + far_query[h * HD : (h + 1) * HD]).T
        rows = raw[:, h * HD : (h + 1) * HD]
        back = unroped(whole, trig[:, :HD], trig[:, HD:])
        inverse = rms_inverse(rows)
        gain_sum = gain_sum + jnp.sum(back * rows * inverse, axis=0, keepdims=True)
        low = rms_backward(back, rows, inverse, consts[0:1])
        o_query[:, h * HD : (h + 1) * HD] = low.astype(BF)
    o_gain[...] = jnp.broadcast_to(gain_sum, (8, HD))


def back_keys(sc, near, far, query_grad, raw, trig, consts, o_qkv, o_gain):
    both = near[...] + far[...].astype(F32)
    rows = raw[...]
    back = unroped(both[:, :HD], trig[:, :HD], trig[:, HD:])
    inverse = rms_inverse(rows)
    gain_sum = jnp.sum(back * rows * inverse, axis=0, keepdims=True)
    o_gain[...] = jnp.broadcast_to(gain_sum, (8, HD))
    o_qkv[:, :256] = query_grad[...]
    o_qkv[:, 256:384] = rms_backward(back, rows, inverse, consts[1:2]).astype(BF)
    o_qkv[:, 384:] = both[:, HD:].astype(BF)


def core_sum(sc, own, got, o_own, *o_low):
    for k in range(4):
        at = slice(k * BLK, (k + 1) * BLK)
        rows = own[at] + got[at].astype(F32)
        if k:
            o_low[k - 1][...] = rows.astype(BF)
        else:
            o_own[...] = rows


def close_middle(sc, own, one, two, three, tokens, gains, o_middle, o_normed):
    middle = own[...] + one[...].astype(F32) + two[...].astype(F32) + three[...].astype(F32)
    middle = middle + tokens[...].astype(F32)
    o_middle[...] = middle
    o_normed[...] = (middle * rms_inverse(middle) * gains[4:5]).astype(BF)


def close_mlp_grad(sc, own, one, two, three, middle, cot, gains, o_grad, o_low):
    grad = own[...] + one[...].astype(F32) + two[...].astype(F32) + three[...].astype(F32)
    rows = middle[...]
    grad = cot[...].astype(F32) + rms_backward(grad, rows, rms_inverse(rows), gains[4:5])
    o_grad[...] = grad
    o_low[...] = grad.astype(BF)


def close_result(sc, own, one, two, three, middle, o_result):
    rows = own[...] + one[...].astype(F32) + two[...].astype(F32) + three[...].astype(F32)
    o_result[...] = from_plane(rows + middle[...]).astype(BF)


def close_tokens(sc, own, one, two, three, grad_middle, tokens, gains, o_grad):
    grad = own[...] + one[...].astype(F32) + two[...].astype(F32) + three[...].astype(F32)
    rows = tokens[...].astype(F32)
    grad = grad_middle[...] + rms_backward(grad, rows, rms_inverse(rows), gains[0:1])
    o_grad[...] = from_plane(grad).astype(BF)


def gather_tokens(rows):
    got = {k: send(rows, x=k) for k in (2, 1, 3)}
    own = jnp.concatenate([rows, got[1], got[2], got[3]])
    return own, send(own, c=1)


def scatter_tokens(sc, own, other):
    low = [((BLK, 1024), BF)] * 3
    total, *low = call(core_sum, [((BLK, 1024), F32)] + low)(
        sc, own, send(other.astype(BF), c=1)
    )
    got = {k: send(low[k - 1], x=k) for k in (2, 1, 3)}
    return (total, got[1], got[2], got[3]), low[0]


def plane_table(k2, k1):
    return pairs(
        ("yl", "c", "yh"), lambda p: {"c": p["yh"], "yl": p["yl"] ^ k2, "yh": p["c"] ^ k1}
    )


def gather_plane(shard):
    axes = ("yl", "c", "yh")
    got = [lax.ppermute(shard, axes, plane_table(k2, k1)) for k2 in range(2) for k1 in range(2)]
    return jnp.concatenate(got)


PLANE = ("yh", "yl", "z")


def swap_shards(value):
    axes = ("c", "yh")
    return lax.ppermute(value, axes, pairs(axes, lambda p: {"c": p["yh"], "yh": p["c"]}))


def scatter_weights(grads, extra=None):
    blocks = grads.astype(BF).reshape(16, 64, -1)
    if extra is not None:
        more = jnp.broadcast_to(extra.astype(BF)[None], (16,) + extra.shape)
        blocks = jnp.concatenate([blocks, more], 1)
    got = jnp.sum(lax.all_to_all(blocks, PLANE, 0, 0).astype(F32), axis=0)
    own = swap_shards(got[:64].astype(BF)).astype(F32)
    return own if extra is None else (own, got[64:])


def shards(
    tokens,
    cotangent,
    w_query,
    w_key,
    w_value,
    w_output,
    w_gate,
    w_up,
    w_down,
    norm_attn,
    norm_mlp,
    query_norm,
    key_norm,
    segment,
    position,
):
    yl, z, x, yh = (lax.axis_index(a) for a in ("yl", "z", "x", "yh"))
    sc = jnp.stack([yl, z, yh, x]).astype(jnp.int32)

    frequency = rope_base ** (-2.0 * np.arange(HD // 2) / HD)
    sign = np.ones(HD // 2)
    consts = jnp.stack(
        [
            query_norm,
            key_norm,
            jnp.asarray(np.concatenate([frequency, frequency]), F32),
            jnp.asarray(np.concatenate([-sign, sign]), F32),
        ]
    )
    consts = jnp.pad(consts, ((0, 4), (0, 0)))

    given = [tokens, cotangent] + [a.reshape(1, -1) for a in (norm_attn, norm_mlp, position)]
    given += [w_query, w_key, w_value, w_output, w_gate, w_up, w_down]
    qkv_shard, rest_shard, payload, rows_in, cot_in, gains = call(
        opening,
        [
            ((64, 512), BF),
            ((64, 1408), BF),
            ((BLK + PAD, 1024), BF),
            ((BLK, 1024), BF),
            ((BLK, 1024), BF),
            ((8, 1024), F32),
        ],
        copied=[(a.shape, a.dtype) for a in given],
    )(sc, *given)

    plane = gather_plane(qkv_shard)
    whole = {k: send(plane, z=k) for k in (1, 3, 2)}
    got = {k: send(payload, x=k) for k in (2, 1, 3)}
    got[2] = after(got[2], whole[1], whole[3])
    own = jnp.concatenate([payload, got[1], got[2], got[3]])
    gathered = own, send(own, c=1)
    whole = jnp.concatenate([plane, whole[1], whole[2], whole[3]])
    w_qkv = call(in_order, [((1024, 512), BF)])(sc, whole)[0]
    rest = lax.all_gather(swap_shards(rest_shard), PLANE, axis=0, tiled=True)
    w_out, w_gu, w_dn = rest[:, :256], rest[:, 256:1024], rest[:, 1024:]

    keys = [
        call(
            project_keys,
            [
                ((ROWS, 1024), BF),
                ((ROWS, 256), BF),
                ((ROWS, HD), F32),
                ((ROWS, 256), F32),
                ((8, ROWS), F32),
            ],
            flops=2 * ROWS * 1024 * 256,
        )(sc, part.reshape(4, BLK + PAD, 1024), w_qkv, consts)
        for part in gathered
    ]
    normed_rows, near_kv, key_raw, trig, marks = zip(*keys)
    far_kv = send(jnp.concatenate(near_kv), yh=1)
    cot_rows = gather_tokens(after(cot_in, gathered[0]))
    far_kv = [far_kv[:ROWS], far_kv[ROWS:]]
    queries, query_raw = zip(
        *[
            call(
                project_queries,
                [((ROWS, 256), BF), ((ROWS, 256), F32)],
                flops=2 * ROWS * 1024 * 256,
            )(sc, rows, w_qkv, consts, after(t, near_kv[1]))
            for rows, t in zip(normed_rows, trig)
        ]
    )
    near = [
        call(attend_near, [((256, ROWS), F32), ((16, ROWS), F32)], flops=8 * ROWS * ROWS * HD)(
            sc, queries[i], near_kv[i], marks[i]
        )
        for i in range(2)
    ]

    def attend_rest(i, *earlier):
        return call(attend_far, [((ROWS, 256), BF), ((16, ROWS), F32)], flops=8 * ROWS * ROWS * HD)(
            sc, queries[i], after(far_kv[i], *earlier), marks[i], *near[i]
        )

    other = attend_rest(1, near[0][1], cot_rows[0])
    other_part = times_transposed(other[0], w_out)
    own = attend_rest(0, other_part)
    attended = [own, other]
    terms, _ = scatter_tokens(sc, times_transposed(own[0], w_out), other_part)
    middle, normed_two = call(close_middle, [((BLK, 1024), F32), ((BLK, 1024), BF)])(
        sc, *terms, rows_in, gains
    )

    mlp_rows = gather_tokens(normed_two)
    grad_active = [matmul(c, w_dn) for c in cot_rows]
    active, grad_gu = [], []
    for rows, grad in zip(mlp_rows, grad_active):
        gate_up = matmul(rows, w_gu)
        gate, up = gate_up[:, :384], gate_up[:, 384:]
        sigmoid = 1.0 / (1.0 + jnp.exp(-gate))
        silu = gate * sigmoid
        active.append((silu * up).astype(BF))
        grad_gu.append(
            jnp.concatenate(
                [
                    (grad * up * sigmoid * (1.0 + gate * (1.0 - sigmoid))).astype(BF),
                    (grad * silu).astype(BF),
                ],
                axis=1,
            )
        )
    terms, sent = scatter_tokens(sc, *[times_transposed(g, w_gu) for g in grad_gu])
    grad_wgu = sum(transposed_times(r, after(g, sent)) for r, g in zip(mlp_rows, grad_gu))
    grad_wdn = sum(transposed_times(r, after(a, sent)) for r, a in zip(cot_rows, active))
    mlp_blocks = jnp.concatenate([grad_wgu, grad_wdn], 1).astype(BF)
    mlp_sum = lax.all_to_all(mlp_blocks.reshape(16, 64, 1152), PLANE, 0, 0)
    mlp_sum = jnp.sum(mlp_sum.astype(F32), axis=0)
    mlp_grads = mlp_sum.astype(BF)
    mlp_grads = swap_shards(mlp_grads).astype(F32)
    grad_middle, grad_low = call(close_mlp_grad, [((BLK, 1024), F32), ((BLK, 1024), BF)])(
        sc, *terms, middle, cot_in, gains
    )
    grad_attn = gather_tokens(grad_low)
    mlp_terms, _ = scatter_tokens(
        sc, *[times_transposed(after(a, grad_attn[0]), w_dn) for a in active]
    )
    result = call(close_result, [((BLK, 1024), BF)])(sc, *mlp_terms, middle)[0]
    gain_two = jnp.sum(grad_wgu * w_gu.astype(F32), axis=1) / gains[4]

    grad_wout = sum(transposed_times(g, a[0]) for g, a in zip(grad_attn, attended))
    grad_attended = [matmul(g, w_out).astype(BF) for g in grad_attn]
    far_back = [
        call(back_far, [((ROWS, 256), BF), ((256, ROWS), F32)], flops=20 * ROWS * ROWS * HD)(
            sc, queries[i], far_kv[i], marks[i], attended[i][1], grad_attended[i], attended[i][0]
        )
        for i in range(2)
    ]
    got = send(jnp.concatenate([b[0] for b in far_back]), yh=1)
    got = [got[:ROWS], got[ROWS:]]
    near_back = [
        call(
            back_near,
            [((ROWS, 256), F32), ((ROWS, 256), BF), ((8, HD), F32)],
            flops=20 * ROWS * ROWS * HD,
        )(
            sc,
            queries[i],
            near_kv[i],
            marks[i],
            attended[i][1],
            grad_attended[i],
            attended[i][0],
            after(far_back[i][1], far_back[1 - i][1], mlp_sum),
            query_raw[i],
            trig[i],
            consts,
        )
        for i in range(2)
    ]
    grad_wq = sum(transposed_times(p, b[1]) for p, b in zip(normed_rows, near_back))

    def close_keys(i, *earlier):
        b = near_back[i]
        return call(back_keys, [((ROWS, 512), BF), ((8, HD), F32)])(
            sc, b[0], after(got[i], *earlier), b[1], key_raw[i], trig[i], consts
        )

    other = close_keys(1, grad_wq, *mlp_terms)
    other_part = times_transposed(other[0], w_qkv)
    own = close_keys(0, other_part)
    final = [own, other]
    terms, sent = scatter_tokens(sc, times_transposed(own[0], w_qkv), other_part)
    grad_tokens = call(close_tokens, [((BLK, 1024), BF)])(
        sc, *terms, grad_middle, rows_in, gains
    )[0]
    grad_wkv = sum(
        transposed_times(p, f[0][:, 256:]) for p, f in zip(normed_rows, final)
    )

    gain_one = jnp.sum(grad_wq * w_qkv[:, :256].astype(F32), axis=1)
    gain_one = (gain_one + jnp.sum(grad_wkv * w_qkv[:, 256:].astype(F32), axis=1)) / gains[0]
    query_gain = sum(b[2][0] for b in near_back)
    key_gain = sum(f[1][0] for f in final)
    sums = jnp.concatenate([gain_one, gain_two, query_gain, key_gain]).reshape(18, 128)
    sums = jnp.pad(sums.reshape(-1), (0, 8 * 768 - 2304)).reshape(8, 768)
    attn_blocks = jnp.concatenate([grad_wq, grad_wkv, grad_wout], 1).astype(BF)
    attn_grads, sums = scatter_weights(
        after(attn_blocks, sent, result), sums + send(sums, c=1)
    )
    sums = sums[:3]
    sums = (sums + send(sums, x=1)) + (send(sums, x=2) + send(sums, x=3))
    sums = sums.reshape(-1)

    def natural(gain):
        return gain.reshape(2, 8, 64).transpose(1, 0, 2).reshape(-1)

    return (
        result,
        grad_tokens,
        attn_grads[:, :256],
        attn_grads[:, 256:384],
        attn_grads[:, 384:512],
        attn_grads[:, 512:],
        mlp_grads[:, :384],
        mlp_grads[:, 384:768],
        mlp_grads[:, 768:],
        natural(sums[:1024]),
        natural(sums[1024:2048]),
        sums[2048:2176],
        sums[2176:2304],
    )


def solution(mesh):
    whole = Mesh(mesh.devices.reshape(2, 4, 2, 4, 2), AXES)
    dp, tensor = ("yl", "z", "c"), ("x", "yh")
    rows, weight = P(dp + tensor, None), P(dp, tensor)
    in_specs = (rows,) * 2 + (weight,) * 7 + (P(),) * 4 + (P(dp + tensor),) * 2
    out_specs = (rows,) * 2 + (weight,) * 7 + (P(),) * 4
    return jax.shard_map(
        shards, mesh=whole, in_specs=in_specs, out_specs=out_specs, check_vma=False
    )
```
